256 devices in a mesh: row: 16 (over z_lo, y), col: 8 (over x, core), cell: 2 (over z_hi).
Axes of the slice: x: 4, y: 4, z: 8 (z_hi: 2, z_lo: 4; z = z_hi * 4 + z_lo), core: 2. Of those that a mesh axis runs over, the one named last changes fastest.
Arguments:
- counts: int32 [8192, 8192], P(('row', 'col'), 'cell'), may hold values from 0 to 108, as said below
- size_factors: float32 [8192], P('cell'), may hold values from 0.3 to 3
- gene_means: float32 [8192], replicated, may hold values from 0.2 to 20
- dispersions: float32 [8192], replicated, may hold values from 0.5 to 50
- block_order: int32 [128], replicated, may hold values from 0 to 127, each once
Outputs:
- correlation: float32 [8192, 8, 1024], P(('row', 'cell'), 'col')
The draws below stay inside these ranges and needn't reach their ends.
Inputs may be any that keep to these rules, and one draw needn't show every extreme that they name: `counts`: each cell's count is a uniform noise of 0 to 15 plus a gene's multiplier of 0 to 3 times one of four shared cell programs of 0 to 31. `block_order`: A permutation of the 128 block ids.
All inputs are finite; a program needn't handle non-finite values.
Results may differ from the reference program's by a relative error of at most 0.0003.
Values may be sent and summed in bfloat16 or wider, within the bound.
No kernel may reach another device: no remote copies, remote signals or barrier semaphores. Data moves between devices by JAX's collectives and lax.ppermute only.
A program may use at most 128 MiB of HBM per device.

```python
import math
import jax
import jax.numpy as jnp
from jax import lax

G = 8192
CELLS = 8192
NBLK = 128
GB = 64
CT = 1024
N_ROW = 16
N_COL = 8


def draw_counts(key, part):
    key = jax.random.fold_in(key, 11)
    key_noise, key_prog, key_pick, key_mult = jax.random.split(key, 4)
    noise = jax.random.randint(key_noise, (G, CELLS), 0, 16, dtype=jnp.int32)
    program = jax.random.randint(key_prog, (4, CELLS), 0, 32, dtype=jnp.int32)
    picked = jax.random.randint(key_pick, (G,), 0, 4, dtype=jnp.int32)
    factor = jax.random.randint(key_mult, (G, 1), 0, 4, dtype=jnp.int32)
    return noise + factor * program[picked]


def block_scale(own_key, shape, pieces, least, high):
    factor_of, own = 1.0, jax.random.fold_in(own_key, 6)
    for position, parts in pieces:
        draws = jnp.exp(jax.random.uniform(jax.random.fold_in(own, position), (parts,), jnp.float32, least / len(pieces), high / len(pieces)))
        factor_of = factor_of * jnp.repeat(draws, shape[position] // parts).reshape([-1 if axis == position else 1 for axis in range(len(shape))])
    return factor_of


def setup_inputs(seed: int = 0) -> dict:
    seeds = jax.random.split(jax.random.key(seed), 6)
    return {
        "counts": draw_counts(jax.random.fold_in(seeds[5], 71), 0),
        "size_factors": jnp.clip(jnp.exp(math.log(3.0) - 2.3025851 * jax.random.uniform(seeds[1], (CELLS,), jnp.float32) ** block_scale(seeds[1], (CELLS,), ((0, 2),), -0.2, 0.2)), 0.3, 3.0),
        "gene_means": jnp.clip(jnp.exp(jax.random.uniform(seeds[2], (G,), jnp.float32, math.log(0.2), math.log(20.0))), 0.2, 20.0),
        "dispersions": jnp.clip(jnp.exp(jax.random.uniform(seeds[3], (G,), jnp.float32, math.log(0.5), math.log(50.0))), 0.5, 50.0),
        "block_order": jax.random.permutation(seeds[4], NBLK).astype(jnp.int32),
    }


def reference(counts, size_factors, gene_means, dispersions, block_order):
    inside = jnp.arange(GB, dtype=jnp.int32)
    atlas = (block_order.astype(jnp.int32)[:, None] * GB + inside[None, :]).reshape(-1)
    mean_gene = gene_means[atlas][:, None]
    disp_gene = dispersions[atlas][:, None]
    expected = mean_gene * size_factors[None, :]
    spread = jnp.sqrt(expected + expected * expected / disp_gene)
    limit = math.sqrt(CELLS)
    resid = jnp.clip((counts.astype(jnp.float32) - expected) / spread, -limit, limit).astype(jnp.bfloat16)
    wide = resid.astype(jnp.float32)
    sums = lax.optimization_barrier(jnp.sum(wide, axis=1))
    squares = lax.optimization_barrier(jnp.sum(wide * wide, axis=1))
    gram = jnp.dot(resid, resid.T, preferred_element_type=jnp.float32)
    mean = sums / CELLS
    inverse = lax.rsqrt(squares / CELLS - mean * mean + 1e-05)
    full = (gram / CELLS - mean[:, None] * mean[None, :]) * inverse[:, None] * inverse[None, :]
    return full.reshape(G, N_ROW, N_COL, GB).transpose(0, 2, 1, 3).reshape(G, N_COL, CT)
```

```python
import functools
import math

import jax
import jax.numpy as jnp
import numpy as np
from jax import lax
from jax.experimental import pallas as pl
from jax.experimental.pallas import tpu as pltpu
from jax.sharding import PartitionSpec as P

AXES = ("row", "col", "cell")
ZL, NY, NX, NC, NH = 4, 4, 4, 2, 2
EPS = 1e-05
FULL = 32767.0
NT = (((1,), (1,)), ((), ()))


def shift(zl=0, y=0, x=0, c=0, h=0):
    dims, step, pairs = (ZL, NY, NX, NC, NH), (zl, y, x, c, h), []
    for i in range(math.prod(dims)):
        at = np.unravel_index(i, dims)
        to = [(int(a) + s) % d for a, s, d in zip(at, step, dims)]
        pairs.append((i, int(np.ravel_multi_index(to, dims))))
    return pairs


def move(value, **steps):
    return lax.ppermute(value, AXES, shift(**steps))


def residuals(counts, size_factors, gene_means, dispersions, block_order):
    blocks = counts.shape[0]
    place = lax.axis_index(("row", "col"))
    first = block_order[place] * blocks
    mean_gene = lax.dynamic_slice_in_dim(gene_means, first, blocks)[:, None]
    disp_gene = lax.dynamic_slice_in_dim(dispersions, first, blocks)[:, None]
    expected = mean_gene * size_factors[None, :]
    spread = jnp.sqrt(expected + expected * expected / disp_gene)
    limit = math.sqrt(size_factors.shape[0] * lax.axis_size("cell"))
    return jnp.clip((counts.astype(jnp.float32) - expected) / spread, -limit, limit).astype(
        jnp.bfloat16
    )


def encode(p):
    root = jnp.minimum(jnp.sqrt(jnp.abs(p)), 1.0) * FULL + 0.5
    return jnp.where(p < 0, -root, root).astype(jnp.int32).astype(jnp.int16)


def decode(q):
    f = q.astype(jnp.int32).astype(jnp.float32)
    return f * jnp.abs(f) * (1.0 / (FULL * FULL))


def lane_sums(parts):
    ones = jnp.ones((8, 128), jnp.float32)
    return lax.dot_general(
        ones, parts, NT, precision=lax.Precision.HIGHEST, preferred_element_type=jnp.float32
    )


def fold(values):
    tiles = [values[:, i : i + 128] for i in range(0, values.shape[1], 128)]
    while len(tiles) > 1:
        tiles = [a + b for a, b in zip(tiles[::2], tiles[1::2])]
    return tiles[0]


def stats_kernel(cells, steps, r_ref, col_ref, lane_ref, s_acc, q_acc):
    k = pl.program_id(0)

    @pl.when(k == 0)
    def _():
        s_acc[...] = jnp.zeros_like(s_acc)
        q_acc[...] = jnp.zeros_like(q_acc)

    wide = r_ref[...].astype(jnp.float32)
    s_acc[...] += fold(wide)
    q_acc[...] += fold(wide * wide)

    @pl.when(k == steps - 1)
    def _():
        s = jnp.sum(s_acc[...], axis=1, keepdims=True) * (1.0 / cells)
        q = jnp.sum(q_acc[...], axis=1, keepdims=True) * (1.0 / cells)
        il = lax.rsqrt(q - s * s + EPS)
        lane = lax.broadcasted_iota(jnp.int32, col_ref.shape, 1)
        col_ref[...] = jnp.where(lane == 0, s, il)
        row = lax.broadcasted_iota(jnp.int32, lane_ref.shape, 0)
        lane_ref[...] = jnp.where(row == 0, lane_sums(s_acc[...]), lane_sums(q_acc[...])) * (
            1.0 / cells
        )


def row_stats(rows):
    n, cells = rows.shape
    steps = 4
    return pl.pallas_call(
        functools.partial(stats_kernel, cells, steps),
        grid=(steps,),
        in_specs=[pl.BlockSpec((n, cells // steps), lambda k: (0, k))],
        out_specs=[pl.BlockSpec((n, 128), lambda k: (0, 0)), pl.BlockSpec((8, n), lambda k: (0, 0))],
        out_shape=[
            jax.ShapeDtypeStruct((n, 128), jnp.float32),
            jax.ShapeDtypeStruct((8, n), jnp.float32),
        ],
        scratch_shapes=[pltpu.VMEM((n, 128), jnp.float32)] * 2,
        cost_estimate=pl.CostEstimate(
            flops=4 * n * cells, bytes_accessed=2 * n * cells, transcendentals=0
        ),
    )(rows)


def tile_kernel(cells, steps, at, r_ref, p0, p1, p2, p3, rs_ref, own, send, cst, cbuf, acc, s_acc, q_acc):
    k = pl.program_id(0)

    @pl.when(k == 0)
    def _():
        acc[...] = jnp.zeros_like(acc)
        s_acc[...] = jnp.zeros_like(s_acc)
        q_acc[...] = jnp.zeros_like(q_acc)

    for i, p in enumerate((p0, p1, p2, p3)):
        cbuf[pl.ds(pl.multiple_of(at[1 + i] * 64, 64), 64), :] = p[...]
    c = cbuf[...]
    acc[...] += lax.dot_general(r_ref[...], c, NT, preferred_element_type=jnp.float32)
    wide = c.astype(jnp.float32)
    s_acc[...] += fold(wide)
    q_acc[...] += fold(wide * wide)

    @pl.when(k == steps - 1)
    def _():
        half = own.shape[0]
        s = lane_sums(s_acc[...]) * (1.0 / cells)
        q = lane_sums(q_acc[...]) * (1.0 / cells)
        row = lax.broadcasted_iota(jnp.int32, cst.shape, 0)
        cst[...] = jnp.where(row == 0, s, q)
        mean = s[0:1, :]
        il = lax.rsqrt(q[0:1, :] - mean * mean + EPS)
        mine = pl.multiple_of(at[0] * half, half)
        other = pl.multiple_of((1 - at[0]) * half, half)
        cov = acc[pl.ds(mine, half), :] * (1.0 / cells) - rs_ref[pl.ds(mine, half), 0:1] * mean
        own[...] = cov
        cov = acc[pl.ds(other, half), :] * (1.0 / cells) - rs_ref[pl.ds(other, half), 0:1] * mean
        send[...] = encode(cov * rs_ref[pl.ds(other, half), 1:2] * il)


def tile(rows, pieces, rstat, half_id, slots):
    n, cells = rows.shape
    steps, half = 4, n // 2
    at = jnp.stack([half_id, *slots]).astype(jnp.int32)
    width = cells // steps
    piece = pl.BlockSpec((64, width), lambda k, at: (0, k))
    fixed = lambda shape: pl.BlockSpec(shape, lambda k, at: (0, 0))
    return pl.pallas_call(
        functools.partial(tile_kernel, cells, steps),
        grid_spec=pltpu.PrefetchScalarGridSpec(
            num_scalar_prefetch=1,
            grid=(steps,),
            in_specs=[pl.BlockSpec((n, width), lambda k, at: (0, k))]
            + [piece] * 4
            + [fixed((n, 128))],
            out_specs=[fixed((half, 256)), fixed((half, 256)), fixed((8, 256))],
            scratch_shapes=[
                pltpu.VMEM((256, width), jnp.bfloat16),
                pltpu.VMEM((n, 256), jnp.float32),
                pltpu.VMEM((256, 128), jnp.float32),
                pltpu.VMEM((256, 128), jnp.float32),
            ],
        ),
        out_shape=[
            jax.ShapeDtypeStruct((half, 256), jnp.float32),
            jax.ShapeDtypeStruct((half, 256), jnp.int16),
            jax.ShapeDtypeStruct((8, 256), jnp.float32),
        ],
        cost_estimate=pl.CostEstimate(
            flops=2 * n * 256 * cells, bytes_accessed=2 * (n + 256) * cells, transcendentals=0
        ),
    )(at, rows, *pieces, rstat)


def merged(mean, mean2, sq, sq2):
    total = 0.5 * (mean + mean2)
    inv = lax.rsqrt(0.5 * (sq + sq2) - total * total + EPS)
    return inv, jnp.sqrt(sq2 - mean2 * mean2 + EPS) * inv, (mean - mean2) * inv


def row_factors(lane, lane2, half_id):
    half = lane.shape[1] // 2
    cut = lambda v, i: lax.dynamic_slice_in_dim(v[i], half_id * half, half)
    three = merged(cut(lane, 0), cut(lane2, 0), cut(lane, 1), cut(lane2, 1))
    return jnp.pad(jnp.stack(three, axis=1), ((0, 0), (0, 125)))


def joined(own, recv, rf, cst, cst2):
    u, v, w = merged(cst[0:1, :], cst2[0:1, :], cst[1:2, :], cst2[1:2, :])
    return (
        0.5 * own * (rf[:, 0:1] * u)
        + 0.5 * decode(recv) * (rf[:, 1:2] * v)
        + 0.25 * (rf[:, 2:3] * w)
    )


def back_kernel(own, recv, rf, cst, cst2, out):
    out[...] = encode(joined(own[...], recv[...], rf[...], cst[...], cst2[...]))


def final_kernel(at, rf, back, *refs):
    out = refs[-1]
    r = rf[...]
    slot = lax.broadcasted_iota(jnp.int32, (1, 256), 1) // 64
    for k in range(4):
        own, recv, cst, cst2 = refs[4 * k : 4 * k + 4]
        value = joined(own[...], recv[...], r, cst[...], cst2[...])
        piece = decode(back[...])[:, 64 * k : 64 * k + 64]
        far = jnp.concatenate([piece] * 4, axis=1)
        where = pl.multiple_of(at[1 + k] * 256, 256)
        out[:, pl.ds(where, 256)] = jnp.where(slot == at[0], far, value)


def local(counts, size_factors, gene_means, dispersions, block_order):
    row, h = lax.axis_index("row"), lax.axis_index("cell")
    zl, y = row // NY, row % NY
    a = residuals(counts, size_factors, gene_means, dispersions, block_order)
    rows = lax.all_gather(a, "col", axis=0, tiled=True)
    z = [a] + [move(a, zl=k) for k in (1, 2, 3)]
    far_rows = lax.all_gather(move(a, y=2), "col", axis=0, tiled=True)
    rstat, rlane = row_stats(rows)
    fstat, flane = row_stats(far_rows)
    rf = row_factors(rlane, move(rlane, h=1), h)
    ff = row_factors(flane, move(flane, h=1), h)

    slots = [(y - 1) % NY, y, (y + 1) % NY, (y + 2) % NY]
    refs = []
    for k in range(ZL):
        pieces = (move(z[k], y=1), z[k], move(z[k], y=-1), z[k])
        own, send, cst = tile(rows, pieces, rstat, h, slots)
        refs += [own, move(send, h=1), cst, move(cst, h=1)]

    own, send, cst = tile(far_rows, z, fstat, h, [jnp.int32(k) for k in range(4)])
    back = pl.pallas_call(
        back_kernel, out_shape=jax.ShapeDtypeStruct(send.shape, jnp.int16)
    )(own, move(send, h=1), ff, cst, move(cst, h=1))
    back = move(back, y=2)

    at = jnp.stack([(y + 2) % NY] + [(zl - k) % ZL for k in range(ZL)]).astype(jnp.int32)
    whole = pl.BlockSpec(memory_space=pltpu.VMEM)
    result = pl.pallas_call(
        final_kernel,
        in_specs=[pl.BlockSpec(memory_space=pltpu.SMEM)] + [whole] * (2 + len(refs)),
        out_specs=whole,
        out_shape=jax.ShapeDtypeStruct((own.shape[0], 1024), jnp.float32),
    )(at, rf, back, *refs)
    return result[:, None, :]


def solution(mesh):
    return jax.shard_map(
        local,
        mesh=mesh,
        in_specs=(P(("row", "col"), "cell"), P("cell"), P(), P(), P()),
        out_specs=P(("row", "cell"), "col", None),
        check_vma=False,
    )
```

```python
import functools
import math

import jax
import jax.numpy as jnp
import numpy as np
from jax import lax
from jax.experimental import pallas as pl
from jax.experimental.pallas import tpu as pltpu
from jax.sharding import PartitionSpec as P

AXES = ("row", "col", "cell")
ZL, NY, NX, NC, NH = 4, 4, 4, 2, 2
EPS = 1e-05
FULL = 32767.0
BOUND = 96.0
NT = (((1,), (1,)), ((), ()))


def shift(zl=0, y=0, x=0, c=0, h=0):
    dims, step, pairs = (ZL, NY, NX, NC, NH), (zl, y, x, c, h), []
    for i in range(math.prod(dims)):
        at = np.unravel_index(i, dims)
        to = [(int(a) + s) % d for a, s, d in zip(at, step, dims)]
        pairs.append((i, int(np.ravel_multi_index(to, dims))))
    return pairs


def move(value, **steps):
    return lax.ppermute(value, AXES, shift(**steps))


def resid_kernel(limit, place, order, counts, size, mean, disp, out, turned):
    genes = out.shape[0]
    block = order[place[0]]
    line = block * genes // 128
    start = pl.multiple_of(block * genes % 128, genes)
    both = [ref[pl.ds(line, 1), :] for ref in (mean, disp)]
    index = lax.broadcasted_iota(jnp.int32, (8, 128), 0)
    turned[...] = jnp.where(index == 0, both[0], both[1]).T
    mean_gene = turned[pl.ds(start, genes), 0:1]
    spare = 1.0 / turned[pl.ds(start, genes), 1:2]
    for i in range(0, out.shape[1], 512):
        span = slice(i, i + 512)
        expected = mean_gene * size[:, span]
        scale = lax.rsqrt(expected + expected * expected * spare)
        value = (counts[:, span].astype(jnp.float32) - expected) * scale
        out[:, span] = jnp.clip(value, -limit, limit).astype(jnp.bfloat16)


def residuals(counts, size_factors, gene_means, dispersions, block_order):
    genes, cells = counts.shape
    place = lax.axis_index(("row", "col")).astype(jnp.int32)
    smem, vmem = pl.BlockSpec(memory_space=pltpu.SMEM), pl.BlockSpec(memory_space=pltpu.VMEM)
    return pl.pallas_call(
        functools.partial(resid_kernel, math.sqrt(cells * NH)),
        in_specs=[smem, smem, vmem, vmem, vmem, vmem],
        out_specs=vmem,
        out_shape=jax.ShapeDtypeStruct((genes, cells), jnp.bfloat16),
        scratch_shapes=[pltpu.VMEM((128, 8), jnp.float32)],
    )(
        place[None],
        block_order,
        counts,
        size_factors[None, :],
        gene_means.reshape(-1, 128),
        dispersions.reshape(-1, 128),
    )


def encode(p):
    root = jnp.minimum(jnp.sqrt(jnp.abs(p)), 1.0) * FULL + 0.5
    return jnp.where(p < 0, -root, root).astype(jnp.int32).astype(jnp.int16)


def decode(q):
    f = q.astype(jnp.int32).astype(jnp.float32)
    return f * jnp.abs(f) * (1.0 / (FULL * FULL))


def split(v):
    t = v * (FULL / BOUND)
    high = jnp.round(t)
    return high, jnp.round((t - high) * (2 * FULL))


def unsplit(high, low):
    return (high + low * (0.5 / FULL)) * (BOUND / FULL)


def pack(rows):
    index = lax.broadcasted_iota(jnp.int32, (16, rows[0].shape[1]), 0)
    block = jnp.zeros(index.shape, jnp.float32)
    for i, row in enumerate(rows):
        block = jnp.where(index == i, row, block)
    return block.astype(jnp.int32).astype(jnp.int16)


def lane_sums(parts):
    ones = jnp.ones((8, 128), jnp.float32)
    return lax.dot_general(
        ones, parts, NT, precision=lax.Precision.HIGHEST, preferred_element_type=jnp.float32
    )[0:1, :]


def fold(values):
    tiles = [values[:, i : i + 128] for i in range(0, values.shape[1], 128)]
    while len(tiles) > 1:
        tiles = [a + b for a, b in zip(tiles[::2], tiles[1::2])]
    return tiles[0]


def deviation(square, mean):
    return jnp.sqrt(square - mean * mean + EPS)


def tile_kernel(cells, steps, count, parts, first, at, *refs):
    refs = list(refs)
    rows = [refs.pop(0) for _ in range(parts)]
    pieces = [refs.pop(0) for _ in range(4 * count)]
    given = None if first else refs.pop(0)
    own, msg, cst = refs.pop(0), refs.pop(0), refs.pop(0)
    rst = refs.pop(0) if first else given
    cbuf, acc, s_acc, q_acc = refs[:4]
    k = pl.program_id(0)
    half = own.shape[0]

    @pl.when(k == 0)
    def _():
        acc[...] = jnp.zeros_like(acc)
        s_acc[...] = jnp.zeros_like(s_acc)
        q_acc[...] = jnp.zeros_like(q_acc)
        if first:
            refs[4][...] = jnp.zeros_like(refs[4])
            refs[5][...] = jnp.zeros_like(refs[5])

    for i, p in enumerate(pieces):
        place = 256 * (i // 4) + at[1 + i] * 64
        cbuf[pl.ds(pl.multiple_of(place, 64), 64), :] = p[...]
    if parts == 1:
        r = rows[0][...]
    else:
        rbuf = refs[6]
        for j, part in enumerate(rows):
            for i in range(part.shape[0] // 64):
                place = at[1 + 4 * count + 4 * j + i] * 64
                rbuf[pl.ds(pl.multiple_of(place, 64), 64), :] = part[64 * i : 64 * i + 64, :]
        r = rbuf[...]
    c = cbuf[...]
    acc[...] += lax.dot_general(r, c, NT, preferred_element_type=jnp.float32)
    wide = c.astype(jnp.float32)
    s_acc[...] += fold(wide)
    q_acc[...] += fold(wide * wide)
    if first:
        wide = r.astype(jnp.float32)
        refs[4][...] += fold(wide)
        refs[5][...] += fold(wide * wide)

    @pl.when(k == steps - 1)
    def _():
        scale = 1.0 / cells
        mine = pl.multiple_of(at[0] * half, half)
        other = pl.multiple_of((1 - at[0]) * half, half)
        extra = []
        if first:
            rs, rq = refs[4], refs[5]
            mean = jnp.sum(rs[...], axis=1, keepdims=True) * scale
            dev = deviation(jnp.sum(rq[...], axis=1, keepdims=True) * scale, mean)
            lane = lax.broadcasted_iota(jnp.int32, rst.shape, 1)
            rst[...] = jnp.where(lane == 0, mean, dev)
            mean = lane_sums(rs[pl.ds(other, half), :]) * scale
            dev = deviation(lane_sums(rq[pl.ds(other, half), :]) * scale, mean)
            extra = [*split(mean), *split(dev)]
        for t in range(count):
            span = slice(256 * t, 256 * t + 256)
            mean = lane_sums(s_acc[span, :]) * scale
            dev = deviation(lane_sums(q_acc[span, :]) * scale, mean)
            row = lax.broadcasted_iota(jnp.int32, (8, 256), 0)
            cst[8 * t : 8 * t + 8, :] = jnp.where(row == 0, mean, dev)
            cov = acc[pl.ds(mine, half), span] * scale - rst[pl.ds(mine, half), 0:1] * mean
            own[:, span] = cov
            cov = acc[pl.ds(other, half), span] * scale - rst[pl.ds(other, half), 0:1] * mean
            base = (half + 16) * t
            msg[base : base + half, :] = encode(
                cov * ((1.0 / rst[pl.ds(other, half), 1:2]) * (1.0 / dev))
            )
            msg[base + half : base + half + 16, :] = pack([*split(mean), *split(dev), *extra])


def tiles(rows, sets, rstat, half_id, slots, places=()):
    n, cells = sum(part.shape[0] for part in rows), rows[0].shape[1]
    steps, half, count = 2, n // 2, len(sets)
    first = rstat is None
    at = jnp.stack([half_id, *slots, *places]).astype(jnp.int32)
    width = cells // steps
    piece = pl.BlockSpec((64, width), lambda k, at: (0, k))
    fixed = lambda shape: pl.BlockSpec(shape, lambda k, at: (0, 0))
    f32 = lambda *shape: jax.ShapeDtypeStruct(shape, jnp.float32)
    outs = [
        f32(half, 256 * count),
        jax.ShapeDtypeStruct(((half + 16) * count, 256), jnp.int16),
        f32(8 * count, 256),
    ]
    scratch = [
        pltpu.VMEM((256 * count, width), jnp.bfloat16),
        pltpu.VMEM((n, 256 * count), jnp.float32),
        pltpu.VMEM((256 * count, 128), jnp.float32),
        pltpu.VMEM((256 * count, 128), jnp.float32),
    ]
    if first:
        outs.append(f32(n, 128))
        scratch += [pltpu.VMEM((n, 128), jnp.float32)] * 2
    if len(rows) > 1:
        scratch.append(pltpu.VMEM((n, width), jnp.bfloat16))
    return pl.pallas_call(
        functools.partial(tile_kernel, cells, steps, count, len(rows), first),
        grid_spec=pltpu.PrefetchScalarGridSpec(
            num_scalar_prefetch=1,
            grid=(steps,),
            in_specs=[pl.BlockSpec((r.shape[0], width), lambda k, at: (0, k)) for r in rows]
            + [piece] * (4 * count)
            + ([] if first else [fixed((n, 128))]),
            out_specs=[fixed(o.shape) for o in outs],
            scratch_shapes=scratch,
        ),
        out_shape=outs,
        compiler_params=pltpu.CompilerParams(vmem_limit_bytes=32 * 1024 * 1024),
        cost_estimate=pl.CostEstimate(
            flops=2 * n * 256 * count * cells, bytes_accessed=2 * (n + 256) * cells, transcendentals=0
        ),
    )(at, *rows, *[p for s in sets for p in s], *([] if first else [rstat]))


def merged(mean, mean2, dev, dev2):
    gap = mean - mean2
    inv = lax.rsqrt(0.5 * (dev * dev + dev2 * dev2) + 0.25 * gap * gap)
    return inv, dev2 * inv, gap * inv


def received(block, i):
    f = block.astype(jnp.int32).astype(jnp.float32)
    return unsplit(f[i : i + 1, :], f[i + 1 : i + 2, :]), unsplit(f[i + 2 : i + 3, :], f[i + 3 : i + 4, :])


def row_factors(rst, block, half_id):
    mean2, dev2 = received(block, 4)
    index = lax.broadcasted_iota(jnp.int32, (8, mean2.shape[1]), 0)
    flip = jnp.where(index == 0, mean2, dev2).T
    half = flip.shape[0]
    mine = pl.multiple_of(half_id * half, half)
    own = rst[pl.ds(mine, half), :]
    return merged(own[:, 0:1], flip[:, 0:1], own[:, 1:2], flip[:, 1:2])


def joined(own, msg, cst, factors):
    half = own.shape[0]
    mean2, dev2 = received(msg[half : half + 16, :], 0)
    u, v, w = merged(cst[0:1, :], mean2, cst[1:2, :], dev2)
    ru, rv, rw = factors
    return (
        0.5 * own * (ru * u) + 0.5 * decode(msg[0:half, :]) * (rv * v) + 0.25 * (rw * w)
    )


def back_kernel(at, own, msg, cst, rst, out):
    half = own.shape[0]
    factors = row_factors(rst, msg[half : half + 16, :], at[0])
    out[...] = encode(joined(own[...], msg[...], cst[...], factors))


def final_kernel(groups, at, rst, back, *refs):
    out = refs[-1]
    slot = lax.broadcasted_iota(jnp.int32, (1, 256), 1) // 64
    half = back.shape[0]
    rows = half + 16
    factors = row_factors(rst, refs[1][half:rows, :], at[0])
    far_all = decode(back[...])
    for g, ids in enumerate(groups):
        own, msg, cst = refs[3 * g : 3 * g + 3]
        for t, k in enumerate(ids):
            value = joined(
                own[:, 256 * t : 256 * t + 256],
                msg[rows * t : rows * t + rows, :],
                cst[8 * t : 8 * t + 8, :],
                factors,
            )
            piece = far_all[:, 64 * k : 64 * k + 64]
            far = jnp.concatenate([piece] * 4, axis=1)
            value = jnp.where(slot == at[1], far, value)
            out[:, at[2 + k] * 2, :] = value[:, 0:128]
            out[:, at[2 + k] * 2 + 1, :] = value[:, 128:256]


def after(value, *others):
    return lax.optimization_barrier((value, *others))[0]


def local(counts, size_factors, gene_means, dispersions, block_order):
    row, col, h = lax.axis_index("row"), lax.axis_index("col"), lax.axis_index("cell")
    zl, y = row // NY, row % NY
    x, c = col // NC, col % NC
    a = residuals(counts, size_factors, gene_means, dispersions, block_order)
    rows = lax.all_gather(a, "col", axis=0, tiled=True)
    z1, z3 = move(a, zl=1), move(a, zl=3)
    up, down = {0: move(a, y=1)}, {0: move(a, y=-1)}
    far = move(a, y=2)
    z2 = move(after(a, z1, z3), zl=2)
    z = [a, z1, z2, z3]
    for k in (1, 3, 2):
        up[k], down[k] = move(z[k], y=1), move(z[k], y=-1)
    far_mine = jnp.concatenate([far, move(far, x=1), move(far, x=-1), move(far, x=2)], axis=0)
    far_theirs = move(far_mine, c=1)

    slots = [(y - 1) % NY, y, (y + 1) % NY, (y + 2) % NY]
    pieces = lambda k: (up[k], z[k], down[k], z[k])
    own01, msg01, cst01, rstat = tiles([rows], [pieces(0), pieces(1)], None, h, slots * 2)
    msg01 = move(msg01, h=1)
    order = [(x - d) % NX * 2 for d in (0, 1, 3, 2)]
    places = [o + c for o in order] + [o + 1 - c for o in order]
    ownf, msgf, cstf, fstat = tiles(
        [far_mine, far_theirs], [z], None, h, [jnp.int32(k) for k in range(4)], places
    )
    msgf = move(msgf, h=1)
    own3, msg3, cst3 = tiles([rows], [pieces(3)], rstat, h, slots)
    msg3 = move(msg3, h=1)
    own2, msg2, cst2 = tiles([rows], [pieces(2)], rstat, h, slots)
    msg2 = move(msg2, h=1)

    whole = pl.BlockSpec(memory_space=pltpu.VMEM)
    smem = pl.BlockSpec(memory_space=pltpu.SMEM)
    half = ownf.shape[0]
    back = pl.pallas_call(
        back_kernel,
        in_specs=[smem] + [whole] * 4,
        out_specs=whole,
        out_shape=jax.ShapeDtypeStruct((half, 256), jnp.int16),
    )(jnp.stack([h]).astype(jnp.int32), ownf, msgf, cstf, fstat)
    back = move(back, y=2)

    at = jnp.stack([h, (y + 2) % NY] + [(zl - k) % ZL for k in range(ZL)]).astype(jnp.int32)
    result = pl.pallas_call(
        functools.partial(final_kernel, ((0, 1), (3,), (2,))),
        in_specs=[smem] + [whole] * 11,
        out_specs=whole,
        out_shape=jax.ShapeDtypeStruct((half, 8, 128), jnp.float32),
    )(at, rstat, back, own01, msg01, cst01, own3, msg3, cst3, own2, msg2, cst2)
    return result.reshape(half, 1, 1024)


def solution(mesh):
    return jax.shard_map(
        local,
        mesh=mesh,
        in_specs=(P(("row", "col"), "cell"), P("cell"), P(), P(), P()),
        out_specs=P(("row", "cell"), "col", None),
        check_vma=False,
    )
```

```python
import functools
import math

import jax
import jax.numpy as jnp
import numpy as np
from jax import lax
from jax.experimental import pallas as pl
from jax.experimental.pallas import tpu as pltpu
from jax.sharding import PartitionSpec as P

AXES = ("row", "col", "cell")
ZL, NY, NX, NC, NH = 4, 4, 4, 2, 2
EPS = 1e-05
FULL = 32767.0
BOUND = 96.0
NT = (((1,), (1,)), ((), ()))


def shift(zl=0, y=0, x=0, c=0, h=0):
    dims, step, pairs = (ZL, NY, NX, NC, NH), (zl, y, x, c, h), []
    for i in range(math.prod(dims)):
        at = np.unravel_index(i, dims)
        to = [(int(a) + s) % d for a, s, d in zip(at, step, dims)]
        pairs.append((i, int(np.ravel_multi_index(to, dims))))
    return pairs


def move(value, **steps):
    return lax.ppermute(value, AXES, shift(**steps))


def resid_kernel(limit, place, order, counts, size, mean, disp, out, turned):
    genes = out.shape[0]
    block = order[place[0]]
    line = block * genes // 128
    start = pl.multiple_of(block * genes % 128, genes)
    both = [ref[pl.ds(line, 1), :] for ref in (mean, disp)]
    index = lax.broadcasted_iota(jnp.int32, (8, 128), 0)
    turned[...] = jnp.where(index == 0, both[0], both[1]).T
    mean_gene = turned[pl.ds(start, genes), 0:1]
    spare = 1.0 / turned[pl.ds(start, genes), 1:2]
    for i in range(0, out.shape[1], 512):
        span = slice(i, i + 512)
        expected = mean_gene * size[:, span]
        scale = lax.rsqrt(expected + expected * expected * spare)
        value = (counts[:, span].astype(jnp.float32) - expected) * scale
        out[:, span] = jnp.clip(value, -limit, limit).astype(jnp.bfloat16)


def residuals(counts, size_factors, gene_means, dispersions, block_order):
    genes, cells = counts.shape
    place = lax.axis_index(("row", "col")).astype(jnp.int32)
    smem, vmem = pl.BlockSpec(memory_space=pltpu.SMEM), pl.BlockSpec(memory_space=pltpu.VMEM)
    return pl.pallas_call(
        functools.partial(resid_kernel, math.sqrt(cells * NH)),
        in_specs=[smem, smem, vmem, vmem, vmem, vmem],
        out_specs=vmem,
        out_shape=jax.ShapeDtypeStruct((genes, cells), jnp.bfloat16),
        scratch_shapes=[pltpu.VMEM((128, 8), jnp.float32)],
    )(
        place[None],
        block_order,
        counts,
        size_factors[None, :],
        gene_means.reshape(-1, 128),
        dispersions.reshape(-1, 128),
    )


def encode(p):
    root = jnp.minimum(jnp.sqrt(jnp.abs(p)), 1.0) * FULL + 0.5
    return jnp.where(p < 0, -root, root).astype(jnp.int32).astype(jnp.int16)


def decode(q):
    f = q.astype(jnp.int32).astype(jnp.float32)
    return f * jnp.abs(f) * (1.0 / (FULL * FULL))


def split(v):
    t = v * (FULL / BOUND)
    high = jnp.round(t)
    return high, jnp.round((t - high) * (2 * FULL))


def unsplit(high, low):
    return (high + low * (0.5 / FULL)) * (BOUND / FULL)


def pack(rows):
    index = lax.broadcasted_iota(jnp.int32, (16, rows[0].shape[1]), 0)
    block = jnp.zeros(index.shape, jnp.float32)
    for i, row in enumerate(rows):
        block = jnp.where(index == i, row, block)
    return block.astype(jnp.int32).astype(jnp.int16)


def lane_sums(parts):
    ones = jnp.ones((8, 128), jnp.float32)
    return lax.dot_general(
        ones, parts, NT, precision=lax.Precision.HIGHEST, preferred_element_type=jnp.float32
    )[0:1, :]


def fold(values):
    tiles = [values[:, i : i + 128] for i in range(0, values.shape[1], 128)]
    while len(tiles) > 1:
        tiles = [a + b for a, b in zip(tiles[::2], tiles[1::2])]
    return tiles[0]


def deviation(square, mean):
    return jnp.sqrt(square - mean * mean + EPS)


def tile_kernel(cells, count, parts, first, at, *refs):
    refs = list(refs)
    rows = [refs.pop(0) for _ in range(parts)]
    pieces = [refs.pop(0) for _ in range(4 * count)]
    given = None if first else refs.pop(0)
    own, msg, cst = refs.pop(0), refs.pop(0), refs.pop(0)
    rst = refs.pop(0) if first else given
    cbuf, acc = refs[:2]
    half = own.shape[0]

    for i, p in enumerate(pieces):
        place = 256 * (i // 4) + at[1 + i] * 64
        cbuf[pl.ds(pl.multiple_of(place, 64), 64), :] = p[...]
    if parts == 1:
        rbuf = rows[0]
    else:
        rbuf = refs[2]
        for j, part in enumerate(rows):
            for i in range(part.shape[0] // 64):
                place = at[1 + 4 * count + 4 * j + i] * 64
                rbuf[pl.ds(pl.multiple_of(place, 64), 64), :] = part[64 * i : 64 * i + 64, :]

    total = sums = squares = row_sums = row_squares = 0.0
    for k in range(0, cells, 1024):
        r, c = rbuf[:, k : k + 1024], cbuf[:, k : k + 1024]
        total += lax.dot_general(r, c, NT, preferred_element_type=jnp.float32)
        wide = c.astype(jnp.float32)
        sums += fold(wide)
        squares += fold(wide * wide)
        if first:
            wide = r.astype(jnp.float32)
            row_sums += fold(wide)
            row_squares += fold(wide * wide)
    acc[...] = total

    scale = 1.0 / cells
    mine = pl.multiple_of(at[0] * half, half)
    other = pl.multiple_of((1 - at[0]) * half, half)
    extra = []
    if first:
        rs, rq = refs[-2:]
        rs[...], rq[...] = row_sums, row_squares
        mean = jnp.sum(row_sums, axis=1, keepdims=True) * scale
        dev = deviation(jnp.sum(row_squares, axis=1, keepdims=True) * scale, mean)
        lane = lax.broadcasted_iota(jnp.int32, rst.shape, 1)
        rst[...] = jnp.where(lane == 0, mean, dev)
        mean = lane_sums(rs[pl.ds(other, half), :]) * scale
        dev = deviation(lane_sums(rq[pl.ds(other, half), :]) * scale, mean)
        extra = [*split(mean), *split(dev)]
    means, devs = lane_sums(sums) * scale, lane_sums(squares) * scale
    devs = deviation(devs, means)
    for t in range(count):
        span = slice(256 * t, 256 * t + 256)
        mean, dev = means[:, span], devs[:, span]
        row = lax.broadcasted_iota(jnp.int32, (8, 256), 0)
        cst[8 * t : 8 * t + 8, :] = jnp.where(row == 0, mean, dev)
        cov = acc[pl.ds(other, half), span] * scale - rst[pl.ds(other, half), 0:1] * mean
        base = (half + 16) * t
        msg[base : base + half, :] = encode(
            cov * ((1.0 / rst[pl.ds(other, half), 1:2]) * (1.0 / dev))
        )
        msg[base + half : base + half + 16, :] = pack([*split(mean), *split(dev), *extra])
        own[:, span] = acc[pl.ds(mine, half), span] * scale - rst[pl.ds(mine, half), 0:1] * mean


VMEM_LIMIT = 32 * 1024 * 1024
VMEM = pl.BlockSpec(memory_space=pltpu.VMEM)
SMEM = pl.BlockSpec(memory_space=pltpu.SMEM)


def call(kernel, outs, scratch, flops, at, *args):
    return pl.pallas_call(
        kernel,
        in_specs=[SMEM] + [VMEM] * len(args),
        out_specs=[VMEM] * len(outs),
        out_shape=[jax.ShapeDtypeStruct(*o) for o in outs],
        scratch_shapes=scratch,
        compiler_params=pltpu.CompilerParams(vmem_limit_bytes=VMEM_LIMIT),
        cost_estimate=pl.CostEstimate(flops=flops, bytes_accessed=1 << 20, transcendentals=0),
    )(jnp.stack(at).astype(jnp.int32), *args)


def tiles(rows, sets, rstat, half_id, slots, places=()):
    n, cells = sum(part.shape[0] for part in rows), rows[0].shape[1]
    half, count, first = n // 2, len(sets), rstat is None
    outs = [
        ((half, 256 * count), jnp.float32),
        (((half + 16) * count, 256), jnp.int16),
        ((8 * count, 256), jnp.float32),
    ]
    scratch = [
        pltpu.VMEM((256 * count, cells), jnp.bfloat16),
        pltpu.VMEM((n, 256 * count), jnp.float32),
    ]
    if len(rows) > 1:
        scratch.append(pltpu.VMEM((n, cells), jnp.bfloat16))
    if first:
        outs.append(((n, 128), jnp.float32))
        scratch += [pltpu.VMEM((n, 128), jnp.float32)] * 2
    kernel = functools.partial(tile_kernel, cells, count, len(rows), first)
    stat = [] if first else [rstat]
    return call(
        kernel,
        outs,
        scratch,
        2 * n * 256 * count * cells,
        [half_id, *slots, *places],
        *rows,
        *[p for s in sets for p in s],
        *stat,
    )


def merged(mean, mean2, dev, dev2):
    gap = mean - mean2
    inv = lax.rsqrt(0.5 * (dev * dev + dev2 * dev2) + 0.25 * gap * gap)
    return inv, dev2 * inv, gap * inv


def received(block, i):
    f = block.astype(jnp.int32).astype(jnp.float32)
    return unsplit(f[i : i + 1, :], f[i + 1 : i + 2, :]), unsplit(f[i + 2 : i + 3, :], f[i + 3 : i + 4, :])


def row_factors(rst, block, half_id):
    mean2, dev2 = received(block, 4)
    index = lax.broadcasted_iota(jnp.int32, (8, mean2.shape[1]), 0)
    flip = jnp.where(index == 0, mean2, dev2).T
    half = flip.shape[0]
    mine = pl.multiple_of(half_id * half, half)
    own = rst[pl.ds(mine, half), :]
    return merged(own[:, 0:1], flip[:, 0:1], own[:, 1:2], flip[:, 1:2])


def joined(own, msg, cst, factors):
    half = own.shape[0]
    mean2, dev2 = received(msg[half : half + 16, :], 0)
    u, v, w = merged(cst[0:1, :], mean2, cst[1:2, :], dev2)
    ru, rv, rw = factors
    return (
        0.5 * own * (ru * u) + 0.5 * decode(msg[0:half, :]) * (rv * v) + 0.25 * (rw * w)
    )


def back_kernel(at, own, msg, cst, rst, out):
    half = own.shape[0]
    factors = row_factors(rst, msg[half : half + 16, :], at[0])
    out[...] = encode(joined(own[...], msg[...], cst[...], factors))


def final_kernel(groups, at, rst, back, *refs):
    out = refs[-1]
    slot = lax.broadcasted_iota(jnp.int32, (1, 256), 1) // 64
    half = back.shape[0]
    rows = half + 16
    factors = row_factors(rst, refs[1][half:rows, :], at[0])
    far_all = decode(back[...])
    for g, ids in enumerate(groups):
        own, msg, cst = refs[3 * g : 3 * g + 3]
        for t, k in enumerate(ids):
            value = joined(
                own[:, 256 * t : 256 * t + 256],
                msg[rows * t : rows * t + rows, :],
                cst[8 * t : 8 * t + 8, :],
                factors,
            )
            piece = far_all[:, 64 * k : 64 * k + 64]
            far = jnp.concatenate([piece] * 4, axis=1)
            value = jnp.where(slot == at[1], far, value)
            out[:, at[2 + k] * 2, :] = value[:, 0:128]
            out[:, at[2 + k] * 2 + 1, :] = value[:, 128:256]


def local(counts, size_factors, gene_means, dispersions, block_order):
    row, col, h = lax.axis_index("row"), lax.axis_index("col"), lax.axis_index("cell")
    zl, y = row // NY, row % NY
    x, c = col // NC, col % NC
    a = residuals(counts, size_factors, gene_means, dispersions, block_order)
    rows = lax.all_gather(a, "col", axis=0, tiled=True)
    hold = lax.optimization_barrier
    up, down = {}, {}
    z1, z3, far = move(a, zl=1), move(a, zl=3), move(a, y=2)
    up[0], down[0] = move(a, y=1), move(a, y=-1)
    a, z1, z3, far, up[0], down[0] = hold((a, z1, z3, far, up[0], down[0]))

    z2 = move(a, zl=2)
    up[1], down[1] = move(z1, y=1), move(z1, y=-1)
    f1, f3 = move(far, x=1), move(far, x=-1)
    z3, far, up[1], down[1], f1, f3 = hold((z3, far, up[1], down[1], f1, f3))

    up[3], down[3] = move(z3, y=1), move(z3, y=-1)
    f2 = move(far, x=2)
    z2, up[3], down[3], f2 = hold((z2, up[3], down[3], f2))

    up[2], down[2] = move(z2, y=1), move(z2, y=-1)
    far_mine = jnp.concatenate([far, f1, f2, f3], axis=0)
    far_theirs = move(far_mine, c=1)
    z = [a, z1, z2, z3]

    slots = [(y - 1) % NY, y, (y + 1) % NY, (y + 2) % NY]
    pieces = lambda k: (up[k], z[k], down[k], z[k])
    own01, msg01, cst01, rstat = tiles([rows], [pieces(0), pieces(1)], None, h, slots * 2)
    msg01 = move(msg01, h=1)
    order = [(x - d) % NX * 2 for d in range(4)]
    places = [o + c for o in order] + [o + 1 - c for o in order]
    ownf, msgf, cstf, fstat = tiles(
        [far_mine, far_theirs], [z], None, h, [jnp.int32(k) for k in range(4)], places
    )
    msgf = move(msgf, h=1)
    own3, msg3, cst3 = tiles([rows], [pieces(3)], rstat, h, slots)
    msg3 = move(msg3, h=1)
    own2, msg2, cst2 = tiles([rows], [pieces(2)], rstat, h, slots)
    msg2 = move(msg2, h=1)

    half = ownf.shape[0]
    (back,) = call(
        back_kernel, [((half, 256), jnp.int16)], [], 1 << 22, [h], ownf, msgf, cstf, fstat
    )
    back = move(back, y=2)

    (result,) = call(
        functools.partial(final_kernel, ((0, 1), (3,), (2,))),
        [((half, 8, 128), jnp.float32)],
        [],
        1 << 24,
        [h, (y + 2) % NY] + [(zl - k) % ZL for k in range(ZL)],
        *(rstat, back, own01, msg01, cst01, own3, msg3, cst3, own2, msg2, cst2),
    )
    return result.reshape(half, 1, 1024)


def solution(mesh):
    return jax.shard_map(
        local,
        mesh=mesh,
        in_specs=(P(("row", "col"), "cell"), P("cell"), P(), P(), P()),
        out_specs=P(("row", "cell"), "col", None),
        check_vma=False,
    )
```

```python
import functools
import math

import jax
import jax.numpy as jnp
import numpy as np
from jax import lax
from jax.experimental import pallas as pl
from jax.experimental.pallas import tpu as pltpu
from jax.sharding import Mesh
from jax.sharding import PartitionSpec as P

AXES = ("z", "y", "x", "core", "cell")
DIMS = (4, 4, 4, 2, 2)
NZ, NY, NX, NC, NH = DIMS
EPS = 1e-05
FULL = 32767.0
BOUND = 96.0
NT = (((1,), (1,)), ((), ()))


def move(value, **steps):
    step, pairs = [steps.get(axis, 0) for axis in AXES], []
    for i in range(math.prod(DIMS)):
        to = [(int(a) + s) % d for a, s, d in zip(np.unravel_index(i, DIMS), step, DIMS)]
        pairs.append((i, int(np.ravel_multi_index(to, DIMS))))
    return lax.ppermute(value, AXES, pairs)


def spread_x(copies):
    return lax.all_to_all(copies, "x", 0, 0, tiled=True)


def resid_kernel(limit, place, order, counts, size, mean, disp, out, copies, turned):
    genes = out.shape[0]
    block = order[place[0]]
    line = block * genes // 128
    start = pl.multiple_of(block * genes % 128, genes)
    both = [ref[pl.ds(line, 1), :] for ref in (mean, disp)]
    index = lax.broadcasted_iota(jnp.int32, (8, 128), 0)
    turned[...] = jnp.where(index == 0, both[0], both[1]).T
    mean_gene = turned[pl.ds(start, genes), 0:1]
    spare = 1.0 / turned[pl.ds(start, genes), 1:2]
    for i in range(0, out.shape[1], 512):
        span = slice(i, i + 512)
        expected = mean_gene * size[:, span]
        scale = lax.rsqrt(expected + expected * expected * spare)
        value = (counts[:, span].astype(jnp.float32) - expected) * scale
        value = jnp.clip(value, -limit, limit).astype(jnp.bfloat16)
        out[:, span] = value
        for j in range(copies.shape[0] // genes):
            copies[genes * j : genes * j + genes, span] = value


def residuals(counts, size_factors, gene_means, dispersions, block_order):
    genes, cells = counts.shape
    place = lax.axis_index(AXES[:4]).astype(jnp.int32)
    smem, vmem = pl.BlockSpec(memory_space=pltpu.SMEM), pl.BlockSpec(memory_space=pltpu.VMEM)
    return pl.pallas_call(
        functools.partial(resid_kernel, math.sqrt(cells * NH)),
        in_specs=[smem, smem, vmem, vmem, vmem, vmem],
        out_specs=[vmem, vmem],
        out_shape=[
            jax.ShapeDtypeStruct((genes, cells), jnp.bfloat16),
            jax.ShapeDtypeStruct((NX * genes, cells), jnp.bfloat16),
        ],
        scratch_shapes=[pltpu.VMEM((128, 8), jnp.float32)],
    )(
        place[None],
        block_order,
        counts,
        size_factors[None, :],
        gene_means.reshape(-1, 128),
        dispersions.reshape(-1, 128),
    )


def encode(p):
    root = jnp.minimum(jnp.sqrt(jnp.abs(p)), 1.0) * FULL + 0.5
    return jnp.where(p < 0, -root, root).astype(jnp.int32).astype(jnp.int16)


def decode(q):
    f = q.astype(jnp.int32).astype(jnp.float32)
    return f * jnp.abs(f) * (1.0 / (FULL * FULL))


def split(v):
    t = v * (FULL / BOUND)
    high = jnp.round(t)
    return high, jnp.round((t - high) * (2 * FULL))


def unsplit(high, low):
    return (high + low * (0.5 / FULL)) * (BOUND / FULL)


def pack(rows):
    index = lax.broadcasted_iota(jnp.int32, (16, rows[0].shape[1]), 0)
    block = jnp.zeros(index.shape, jnp.float32)
    for i, row in enumerate(rows):
        block = jnp.where(index == i, row, block)
    return block.astype(jnp.int32).astype(jnp.int16)


def lane_sums(parts):
    ones = jnp.ones((8, 128), jnp.float32)
    return lax.dot_general(
        ones, parts, NT, precision=lax.Precision.HIGHEST, preferred_element_type=jnp.float32
    )[0:1, :]


def fold(values):
    tiles = [values[:, i : i + 128] for i in range(0, values.shape[1], 128)]
    while len(tiles) > 1:
        tiles = [a + b for a, b in zip(tiles[::2], tiles[1::2])]
    return tiles[0]


def deviation(square, mean):
    return jnp.sqrt(square - mean * mean + EPS)


def tile_kernel(cells, count, first, at, *refs):
    refs = list(refs)
    rows = refs[:2]
    pieces = refs[2 : 2 + 4 * count]
    refs = refs[2 + 4 * count :]
    given = None if first else refs.pop(0)
    own, msg, cst = refs.pop(0), refs.pop(0), refs.pop(0)
    rst = refs.pop(0) if first else given
    cbuf, acc = refs[:2]
    half = own.shape[0]

    for i, p in enumerate(pieces):
        place = 256 * (i // 4) + at[2 + i] * 64
        cbuf[pl.ds(pl.multiple_of(place, 64), 64), :] = p[...]

    total = sums = squares = row_sums = row_squares = 0.0
    for k in range(0, cells, 1024):
        c = cbuf[:, k : k + 1024]
        r = jnp.concatenate([part[:, k : k + 1024] for part in rows], axis=0)
        total += lax.dot_general(r, c, NT, preferred_element_type=jnp.float32)
        wide = c.astype(jnp.float32)
        sums += fold(wide)
        squares += fold(wide * wide)
        if first:
            wide = r.astype(jnp.float32)
            row_sums += fold(wide)
            row_squares += fold(wide * wide)
    for i in range(NX * NC):
        core = at[1] if i < NX else 1 - at[1]
        span = pl.ds(pl.multiple_of((NC * (i % NX) + core) * 64, 64), 64)
        acc[span, :] = total[64 * i : 64 * i + 64, :]
        if first:
            refs[-2][span, :] = row_sums[64 * i : 64 * i + 64, :]
            refs[-1][span, :] = row_squares[64 * i : 64 * i + 64, :]

    scale = 1.0 / cells
    mine = pl.multiple_of(at[0] * half, half)
    other = pl.multiple_of((1 - at[0]) * half, half)
    extra = []
    if first:
        rs, rq = refs[-2:]
        mean = jnp.sum(rs[...], axis=1, keepdims=True) * scale
        dev = deviation(jnp.sum(rq[...], axis=1, keepdims=True) * scale, mean)
        lane = lax.broadcasted_iota(jnp.int32, rst.shape, 1)
        rst[...] = jnp.where(lane == 0, mean, dev)
        mean = lane_sums(rs[pl.ds(other, half), :]) * scale
        dev = deviation(lane_sums(rq[pl.ds(other, half), :]) * scale, mean)
        extra = [*split(mean), *split(dev)]
    means, devs = lane_sums(sums) * scale, lane_sums(squares) * scale
    devs = deviation(devs, means)
    for t in range(count):
        span = slice(256 * t, 256 * t + 256)
        mean, dev = means[:, span], devs[:, span]
        row = lax.broadcasted_iota(jnp.int32, (8, 256), 0)
        cst[8 * t : 8 * t + 8, :] = jnp.where(row == 0, mean, dev)
        cov = acc[pl.ds(other, half), span] * scale - rst[pl.ds(other, half), 0:1] * mean
        base = (half + 16) * t
        msg[base : base + half, :] = encode(
            cov * ((1.0 / rst[pl.ds(other, half), 1:2]) * (1.0 / dev))
        )
        msg[base + half : base + half + 16, :] = pack([*split(mean), *split(dev), *extra])
        own[:, span] = acc[pl.ds(mine, half), span] * scale - rst[pl.ds(mine, half), 0:1] * mean


VMEM_LIMIT = 24 * 1024 * 1024
VMEM = pl.BlockSpec(memory_space=pltpu.VMEM)
SMEM = pl.BlockSpec(memory_space=pltpu.SMEM)


def call(kernel, outs, scratch, flops, at, *args):
    return pl.pallas_call(
        kernel,
        in_specs=[SMEM] + [VMEM] * len(args),
        out_specs=[VMEM] * len(outs),
        out_shape=[jax.ShapeDtypeStruct(*o) for o in outs],
        scratch_shapes=scratch,
        compiler_params=pltpu.CompilerParams(vmem_limit_bytes=VMEM_LIMIT),
        cost_estimate=pl.CostEstimate(flops=flops, bytes_accessed=1 << 20, transcendentals=0),
    )(jnp.stack(at).astype(jnp.int32), *args)


def tiles(rows, sets, rstat, half_id, core, slots):
    n, cells = sum(part.shape[0] for part in rows), rows[0].shape[1]
    half, count, first = n // 2, len(sets), rstat is None
    outs = [
        ((half, 256 * count), jnp.float32),
        (((half + 16) * count, 256), jnp.int16),
        ((8 * count, 256), jnp.float32),
    ]
    scratch = [
        pltpu.VMEM((256 * count, cells), jnp.bfloat16),
        pltpu.VMEM((n, 256 * count), jnp.float32),
    ]
    if first:
        outs.append(((n, 128), jnp.float32))
        scratch += [pltpu.VMEM((n, 128), jnp.float32)] * 2
    return call(
        functools.partial(tile_kernel, cells, count, first),
        outs,
        scratch,
        2 * n * 256 * count * cells,
        [half_id, core, *slots],
        *rows,
        *[p for s in sets for p in s],
        *([] if first else [rstat]),
    )


def copies_kernel(at, top, bottom, out):
    n = top.shape[0]
    for i in range(NX):
        out[2 * n * i : 2 * n * i + n, :] = top[...]
        out[2 * n * i + n : 2 * n * i + 2 * n, :] = bottom[...]


def merged(mean, mean2, dev, dev2):
    gap = mean - mean2
    inv = lax.rsqrt(0.5 * (dev * dev + dev2 * dev2) + 0.25 * gap * gap)
    return inv, dev2 * inv, gap * inv


def received(block, i):
    f = block.astype(jnp.int32).astype(jnp.float32)
    return unsplit(f[i : i + 1, :], f[i + 1 : i + 2, :]), unsplit(f[i + 2 : i + 3, :], f[i + 3 : i + 4, :])


def row_factors(rst, block, half_id):
    mean2, dev2 = received(block, 4)
    index = lax.broadcasted_iota(jnp.int32, (8, mean2.shape[1]), 0)
    flip = jnp.where(index == 0, mean2, dev2).T
    half = flip.shape[0]
    mine = pl.multiple_of(half_id * half, half)
    own = rst[pl.ds(mine, half), :]
    return merged(own[:, 0:1], flip[:, 0:1], own[:, 1:2], flip[:, 1:2])


def joined(own, msg, cst, factors):
    half = own.shape[0]
    mean2, dev2 = received(msg[half : half + 16, :], 0)
    u, v, w = merged(cst[0:1, :], mean2, cst[1:2, :], dev2)
    ru, rv, rw = factors
    return (
        0.5 * own * (ru * u) + 0.5 * decode(msg[0:half, :]) * (rv * v) + 0.25 * (rw * w)
    )


def back_kernel(at, own, msg, cst, rst, out):
    half = own.shape[0]
    factors = row_factors(rst, msg[half : half + 16, :], at[0])
    out[...] = encode(joined(own[...], msg[...], cst[...], factors))


def final_kernel(groups, at, rst, back, *refs):
    out = refs[-1]
    slot = lax.broadcasted_iota(jnp.int32, (1, 256), 1) // 64
    half = back.shape[0]
    rows = half + 16
    factors = row_factors(rst, refs[1][half:rows, :], at[0])
    far_all = decode(back[...])
    for g, ids in enumerate(groups):
        own, msg, cst = refs[3 * g : 3 * g + 3]
        for t, k in enumerate(ids):
            value = joined(
                own[:, 256 * t : 256 * t + 256],
                msg[rows * t : rows * t + rows, :],
                cst[8 * t : 8 * t + 8, :],
                factors,
            )
            piece = far_all[:, 64 * k : 64 * k + 64]
            far = jnp.concatenate([piece] * 4, axis=1)
            value = jnp.where(slot == at[1], far, value)
            out[:, at[2 + k] * 2, :] = value[:, 0:128]
            out[:, at[2 + k] * 2 + 1, :] = value[:, 128:256]


def local(counts, size_factors, gene_means, dispersions, block_order):
    zl, y, c, h = [lax.axis_index(axis) for axis in ("z", "y", "core", "cell")]
    hold = lax.optimization_barrier
    up, down = {}, {}
    a, copies = residuals(counts, size_factors, gene_means, dispersions, block_order)
    half = a.shape[0] // 2

    up[0], down[0], z1 = move(a, y=1), move(a, y=-1), move(a, z=1)
    up[0], down[0], z1 = hold((up[0], down[0], z1))

    rows = spread_x(copies)
    z2 = move(z1, z=1)
    far = move(up[0][:half], y=1), move(down[0][half:], y=-1)
    a, rows, z1, z2, *far = hold((a, rows, z1, z2, *far))

    (far,) = call(copies_kernel, [(copies.shape, a.dtype)], [], 1 << 20, [h], *far)
    up[1], down[1] = move(z1, y=1), move(z1, y=-1)
    z3 = move(a, z=3)
    rows = rows, move(rows, core=1)
    z2, z3, up[1], down[1], *rows = hold((z2, z3, up[1], down[1], *rows))

    slots = [(y - 1) % NY, y, (y + 1) % NY, (y + 2) % NY]
    pieces = lambda k: (up[k], z[k], down[k], z[k])
    z = [a, z1, z2, z3]
    up[2], down[2] = move(z2, y=1), move(z2, y=-1)
    own01, msg01, cst01, rstat = tiles(rows, [pieces(0), pieces(1)], None, h, c, slots * 2)
    far = spread_x(far)
    z3, up[2], down[2], far, msg01 = hold((z3, up[2], down[2], far, msg01))

    up[3], down[3] = move(z3, y=1), move(z3, y=-1)
    far = far, move(far, core=1)
    msg01 = move(msg01, cell=1)
    own2, msg2, cst2 = tiles(rows, [pieces(2)], rstat, h, c, slots)
    msg2 = move(msg2, cell=1)
    ownf, msgf, cstf, fstat = tiles(far, [z], None, h, c, [jnp.int32(k) for k in range(NZ)])
    msgf = move(msgf, cell=1)
    own3, msg3, cst3 = tiles(rows, [pieces(3)], rstat, h, c, slots)
    msg3 = move(msg3, cell=1)

    half = ownf.shape[0]
    (back,) = call(
        back_kernel, [((half, 256), jnp.int16)], [], 1 << 22, [h], ownf, msgf, cstf, fstat
    )
    back = move(back, y=2)

    (result,) = call(
        functools.partial(final_kernel, ((0, 1), (2,), (3,))),
        [((half, 8, 128), jnp.float32)],
        [],
        1 << 24,
        [h, (y + 2) % NY] + [(zl - k) % NZ for k in range(NZ)],
        *(rstat, back, own01, msg01, cst01, own2, msg2, cst2, own3, msg3, cst3),
    )
    return result.reshape(half, 1, 1024)


def solution(mesh):
    fine = Mesh(mesh.devices.reshape(DIMS), AXES)
    return jax.shard_map(
        local,
        mesh=fine,
        in_specs=(P(AXES[:4], "cell"), P("cell"), P(), P(), P()),
        out_specs=P(("z", "y", "cell"), ("x", "core"), None),
        check_vma=False,
    )
```

```python
import functools
import math

import jax
import jax.numpy as jnp
import numpy as np
from jax import lax
from jax.experimental import pallas as pl
from jax.experimental.pallas import tpu as pltpu
from jax.sharding import Mesh
from jax.sharding import PartitionSpec as P

AXES = ("z", "y", "x", "core", "cell")
DIMS = (4, 4, 4, 2, 2)
NZ, NY, NX, NC, NH = DIMS
EPS = 1e-05
FULL = 32767.0
BOUND = 96.0
NT = (((1,), (1,)), ((), ()))


def move(value, **steps):
    step, pairs = [steps.get(axis, 0) for axis in AXES], []
    for i in range(math.prod(DIMS)):
        to = [(int(a) + s) % d for a, s, d in zip(np.unravel_index(i, DIMS), step, DIMS)]
        pairs.append((i, int(np.ravel_multi_index(to, DIMS))))
    return lax.ppermute(value, AXES, pairs)


def spread_x(copies):
    return lax.all_to_all(copies, "x", 0, 0, tiled=True)


def resid_kernel(limit, place, order, counts, size, mean, disp, out, copies, turned):
    genes = out.shape[0]
    block = order[place[0]]
    line = block * genes // 128
    start = pl.multiple_of(block * genes % 128, genes)
    both = [ref[pl.ds(line, 1), :] for ref in (mean, disp)]
    index = lax.broadcasted_iota(jnp.int32, (8, 128), 0)
    turned[...] = jnp.where(index == 0, both[0], both[1]).T
    mean_gene = turned[pl.ds(start, genes), 0:1]
    spare = 1.0 / turned[pl.ds(start, genes), 1:2]
    for i in range(0, out.shape[1], 512):
        span = slice(i, i + 512)
        expected = mean_gene * size[:, span]
        scale = lax.rsqrt(expected + expected * expected * spare)
        value = (counts[:, span].astype(jnp.float32) - expected) * scale
        value = jnp.clip(value, -limit, limit).astype(jnp.bfloat16)
        out[:, span] = value
        for j in range(NX):
            copies[genes * j : genes * j + genes, span] = value


def residuals(counts, size_factors, gene_means, dispersions, block_order):
    genes, cells = counts.shape
    place = lax.axis_index(AXES[:4]).astype(jnp.int32)
    smem, vmem = pl.BlockSpec(memory_space=pltpu.SMEM), pl.BlockSpec(memory_space=pltpu.VMEM)
    return pl.pallas_call(
        functools.partial(resid_kernel, math.sqrt(cells * NH)),
        in_specs=[smem, smem, vmem, vmem, vmem, vmem],
        out_specs=[vmem, vmem],
        out_shape=[
            jax.ShapeDtypeStruct((genes, cells), jnp.bfloat16),
            jax.ShapeDtypeStruct((NX * genes, cells), jnp.bfloat16),
        ],
        scratch_shapes=[pltpu.VMEM((128, 8), jnp.float32)],
        compiler_params=pltpu.CompilerParams(vmem_limit_bytes=VMEM_LIMIT),
    )(
        place[None],
        block_order,
        counts,
        size_factors[None, :],
        gene_means.reshape(-1, 128),
        dispersions.reshape(-1, 128),
    )


def encode(p):
    root = jnp.minimum(jnp.sqrt(jnp.abs(p)), 1.0) * FULL + 0.5
    return jnp.where(p < 0, -root, root).astype(jnp.int32).astype(jnp.int16)


def decode(q):
    f = q.astype(jnp.int32).astype(jnp.float32)
    return f * jnp.abs(f) * (1.0 / (FULL * FULL))


def split(v):
    t = v * (FULL / BOUND)
    high = jnp.round(t)
    return high, jnp.round((t - high) * (2 * FULL))


def unsplit(high, low):
    return (high + low * (0.5 / FULL)) * (BOUND / FULL)


def pack(rows):
    index = lax.broadcasted_iota(jnp.int32, (16, rows[0].shape[1]), 0)
    block = jnp.zeros(index.shape, jnp.float32)
    for i, row in enumerate(rows):
        block = jnp.where(index == i, row, block)
    return block.astype(jnp.int32).astype(jnp.int16)


def lane_sums(parts):
    ones = jnp.ones((8, 128), jnp.float32)
    return lax.dot_general(
        ones, parts, NT, precision=lax.Precision.HIGHEST, preferred_element_type=jnp.float32
    )[0:1, :]


def fold(values):
    tiles = [values[:, i : i + 128] for i in range(0, values.shape[1], 128)]
    while len(tiles) > 1:
        tiles = [a + b for a, b in zip(tiles[::2], tiles[1::2])]
    return tiles[0]


def deviation(square, mean):
    return jnp.sqrt(square - mean * mean + EPS)


def tile_kernel(cells, chunks, count, pieces, parts, first, export, at, *refs):
    refs = list(refs)
    blocks = [refs.pop(0) for _ in range(pieces)]
    rows = [refs.pop(0) for _ in range(1 + parts[-1][0] if parts else 1)]
    given = None if first else refs.pop(0)
    own, msg, cst = refs.pop(0), refs.pop(0), refs.pop(0)
    rst = refs.pop(0) if first else given
    ordered = refs.pop(0) if export else None
    rbuf = refs.pop(0) if parts else rows[0]
    cbuf, acc, sems = refs[:3]
    half = own.shape[0]
    width = cells // chunks
    block_at = [pl.ds(pl.multiple_of(at[1 + i] * 32, 64), 64) for i in range(pieces)]

    def copies(k):
        cells_k = pl.ds(width * k, width)
        pairs = [(p.at[:, cells_k], cbuf.at[span, cells_k]) for p, span in zip(blocks, block_at)]
        for i, (ref, start, size) in enumerate(parts):
            span = pl.ds(pl.multiple_of(at[1 + pieces + i] * 32, 32), size)
            pairs.append((rows[ref].at[pl.ds(start, size), cells_k], rbuf.at[span, cells_k]))
        made = [pltpu.make_async_copy(*pair, sems.at[k, i]) for i, pair in enumerate(pairs)]
        for copy in made:
            copy.start()
        return made

    flight = [copies(0), copies(1)] if parts else [[]] * chunks
    if not parts:
        for p, span in zip(blocks, block_at):
            cbuf[span, :] = p[...]
    if pieces < 4 * count:
        for t in range(count):
            span = pl.ds(pl.multiple_of(at[1 + pieces + len(parts) + t] * 32, 64), 64)
            cbuf[span, :] = jnp.zeros((64, cells), cbuf.dtype)
    total = sums = squares = row_sums = row_squares = 0.0
    for k in range(chunks):
        for copy in flight[k]:
            copy.wait()
        if parts and k + 2 < chunks:
            flight.append(copies(k + 2))
        cells_k = slice(width * k, width * k + width)
        r, c = rbuf[:, cells_k], cbuf[:, cells_k]
        total += lax.dot_general(r, c, NT, preferred_element_type=jnp.float32)
        wide = c.astype(jnp.float32)
        sums += fold(wide)
        squares += fold(wide * wide)
        if first:
            wide = r.astype(jnp.float32)
            row_sums += fold(wide)
            row_squares += fold(wide * wide)
    if export:
        out = pltpu.make_async_copy(rbuf, ordered, sems.at[0, 0])
        out.start()
    acc[...] = total
    if first:
        refs[-2][...] = row_sums
        refs[-1][...] = row_squares

    scale = 1.0 / cells
    mine = pl.multiple_of(at[0] * half, half)
    other = pl.multiple_of((1 - at[0]) * half, half)
    extra = []
    if first:
        rs, rq = refs[-2:]
        mean = jnp.sum(rs[...], axis=1, keepdims=True) * scale
        dev = deviation(jnp.sum(rq[...], axis=1, keepdims=True) * scale, mean)
        lane = lax.broadcasted_iota(jnp.int32, rst.shape, 1)
        rst[...] = jnp.where(lane == 0, mean, dev)
        mean = lane_sums(rs[pl.ds(other, half), :]) * scale
        dev = deviation(lane_sums(rq[pl.ds(other, half), :]) * scale, mean)
        extra = [*split(mean), *split(dev)]
    means, devs = lane_sums(sums) * scale, lane_sums(squares) * scale
    devs = deviation(devs, means)
    for t in range(count):
        span = slice(256 * t, 256 * t + 256)
        mean, dev = means[:, span], devs[:, span]
        row = lax.broadcasted_iota(jnp.int32, (8, 256), 0)
        cst[8 * t : 8 * t + 8, :] = jnp.where(row == 0, mean, dev)
        cov = acc[pl.ds(other, half), span] * scale - rst[pl.ds(other, half), 0:1] * mean
        base = (half + 16) * t
        msg[base : base + half, :] = encode(
            cov * ((1.0 / rst[pl.ds(other, half), 1:2]) * (1.0 / dev))
        )
        msg[base + half : base + half + 16, :] = pack([*split(mean), *split(dev), *extra])
        own[:, span] = acc[pl.ds(mine, half), span] * scale - rst[pl.ds(mine, half), 0:1] * mean
    if export:
        out.wait()


VMEM_LIMIT = 60 * 1024 * 1024
VMEM = pl.BlockSpec(memory_space=pltpu.VMEM)
SMEM = pl.BlockSpec(memory_space=pltpu.SMEM)
HBM = pl.BlockSpec(memory_space=pltpu.HBM)


class From:
    def __init__(self, table, first):
        self.table, self.first = table, first

    def __getitem__(self, i):
        return self.table[self.first + i]


def call(kernel, outs, scratch, flops, at, *args, places=None, out_places=None, limit=32 * 1024 * 1024):
    table, first = at
    return pl.pallas_call(
        lambda table, *refs: kernel(From(table, first), *refs),
        in_specs=[SMEM] + (places or [VMEM] * len(args)),
        out_specs=out_places or [VMEM] * len(outs),
        out_shape=[jax.ShapeDtypeStruct(*o) for o in outs],
        scratch_shapes=scratch,
        compiler_params=pltpu.CompilerParams(vmem_limit_bytes=limit or VMEM_LIMIT),
        cost_estimate=pl.CostEstimate(flops=flops, bytes_accessed=1 << 20, transcendentals=0),
    )(table, *args)


def tiles(rows, sets, rstat, at, empty=False, export=False):
    rows, parts = rows
    n, cells = sum(part.shape[0] for part in rows), rows[0].shape[1]
    half, count, first, chunks = n // 2, len(sets), rstat is None, 4
    pieces = [p for s in sets for p in s]
    outs = [
        ((half, 256 * count), jnp.float32),
        (((half + 16) * count, 256), jnp.int16),
        ((8 * count, 256), jnp.float32),
    ]
    out_places = [VMEM] * 3
    scratch = [pltpu.VMEM((n, cells), jnp.bfloat16)] if parts else []
    scratch += [
        pltpu.VMEM((256 * count, cells), jnp.bfloat16),
        pltpu.VMEM((n, 256 * count), jnp.float32),
        pltpu.SemaphoreType.DMA((chunks, len(pieces) + len(parts))),
    ]
    if first:
        outs.append(((n, 128), jnp.float32))
        out_places.append(VMEM)
        scratch += [pltpu.VMEM((n, 128), jnp.float32)] * 2
    if export:
        outs.append(((n, cells), jnp.bfloat16))
        out_places.append(HBM)
    return call(
        functools.partial(tile_kernel, cells, chunks, count, len(pieces), parts, first, export),
        outs,
        scratch,
        int(1.15e9 * (2.5 + 1.5 * count + (3.5 if parts else 0))),
        at,
        *pieces,
        *rows,
        *([] if first else [rstat]),
        places=[HBM if parts else VMEM] * (len(rows) + len(pieces)) + ([] if first else [VMEM]),
        out_places=out_places,
        limit=VMEM_LIMIT if parts else 32 * 1024 * 1024,
    )


def merged(mean, mean2, dev, dev2):
    gap = mean - mean2
    inv = lax.rsqrt(0.5 * (dev * dev + dev2 * dev2) + 0.25 * gap * gap)
    return inv, dev2 * inv, gap * inv


def received(block, i):
    f = block.astype(jnp.int32).astype(jnp.float32)
    return unsplit(f[i : i + 1, :], f[i + 1 : i + 2, :]), unsplit(f[i + 2 : i + 3, :], f[i + 3 : i + 4, :])


def row_factors(rst, block, half_id):
    mean2, dev2 = received(block, 4)
    index = lax.broadcasted_iota(jnp.int32, (8, mean2.shape[1]), 0)
    flip = jnp.where(index == 0, mean2, dev2).T
    half = flip.shape[0]
    mine = pl.multiple_of(half_id * half, half)
    own = rst[pl.ds(mine, half), :]
    return merged(own[:, 0:1], flip[:, 0:1], own[:, 1:2], flip[:, 1:2])


def joined(own, msg, cst, factors):
    half = own.shape[0]
    mean2, dev2 = received(msg[half : half + 16, :], 0)
    u, v, w = merged(cst[0:1, :], mean2, cst[1:2, :], dev2)
    ru, rv, rw = factors
    return (
        0.5 * own * (ru * u) + 0.5 * decode(msg[0:half, :]) * (rv * v) + 0.25 * (rw * w)
    )


def back_kernel(at, own, msg, cst, rst, out):
    half = own.shape[0]
    factors = row_factors(rst, msg[half : half + 16, :], at[0])
    out[...] = encode(joined(own[...], msg[...], cst[...], factors))


def final_kernel(groups, at, rst, back, *refs):
    out = refs[-1]
    slot = lax.broadcasted_iota(jnp.int32, (1, 256), 1) // 64
    half = back.shape[0]
    rows = half + 16
    factors = row_factors(rst, refs[1][half:rows, :], at[0])
    far_all = decode(back[...])
    for g, ids in enumerate(groups):
        own, msg, cst = refs[3 * g : 3 * g + 3]
        for t, k in enumerate(ids):
            value = joined(
                own[:, 256 * t : 256 * t + 256],
                msg[rows * t : rows * t + rows, :],
                cst[8 * t : 8 * t + 8, :],
                factors,
            )
            piece = far_all[:, 64 * k : 64 * k + 64]
            far = jnp.concatenate([piece] * 4, axis=1)
            value = jnp.where(slot == at[1], far, value)
            out[:, at[2 + k] * 2, :] = value[:, 0:128]
            out[:, at[2 + k] * 2 + 1, :] = value[:, 128:256]


def local(counts, size_factors, gene_means, dispersions, block_order):
    zl, y, x, c, h = [lax.axis_index(axis) for axis in AXES]
    hold = lax.optimization_barrier
    up, down = {}, {}
    near, last = [(y - 1) % NY * 2, y * 2, (y + 1) % NY * 2], (y + 2) % NY * 2
    place = lambda at, core: 2 * (NC * (at % NX) + core)
    row_places = [place(i, core) for core in (c, 1 - c) for i in range(NX)]
    lists = [
        [h, *near, *[8 + i for i in near]] + row_places + [last, 8 + last],
        [h, *near, *[8 + i for i in near], last, 8 + last],
        [h, *[2 * k for k in range(NZ)]]
        + [place(x + d, core) for core in (c, 1 - c) for d in (0, -1, 1, 2)],
        [h, (y + 2) % NY] + [(zl - k) % NZ for k in range(NZ)],
    ]
    table = jnp.stack([jnp.asarray(v, jnp.int32) for values in lists for v in values])
    starts = np.cumsum([0] + [len(values) for values in lists]).tolist()
    at_one, at_two, at_far, at_end = [(table, start) for start in starts[:4]]

    a, copies = residuals(counts, size_factors, gene_means, dispersions, block_order)

    up[0], down[0], z1, far = move(a, y=1), move(a, y=-1), move(a, z=1), move(a, y=2)
    z3 = move(a, z=3)
    rows = spread_x(copies)
    up[0], down[0], z1, z3, far = hold((up[0], down[0], z1, z3, far))

    up[1], down[1], z2 = move(z1, y=1), move(z1, y=-1), move(z1, z=1)
    far, far_c = hold((far, move(far, core=1)))
    right, left = move(far, x=1), move(far, x=-1)
    rows, z2, up[1], down[1], right, left = hold((rows, z2, up[1], down[1], right, left))

    pieces = lambda k: (up[k], z[k], down[k])
    up[2], down[2] = move(z2, y=1), move(z2, y=-1)
    z = [a, z1, z2, z3]
    rows_c = move(rows, core=1)
    across = move(far, x=2)
    rows = (rows, rows_c), [(i // NX, 64 * (i % NX), 64) for i in range(2 * NX)]
    own01, msg01, cst01, rstat, ordered = tiles(
        rows, [pieces(0), pieces(1)], None, at_one, True, True
    )
    z3, up[2], down[2], own01, across = hold((z3, up[2], down[2], own01, across))

    z = [a, z1, z2, z3]
    up[3], down[3] = move(z3, y=1), move(z3, y=-1)
    across_c, right_c, left_c = move(across, core=1), move(right, core=1), move(left, core=1)
    msg01 = move(msg01, cell=1)
    far = [far, right, left, across, far_c, right_c, left_c, across_c]
    far = far, [(i, 0, part.shape[0]) for i, part in enumerate(far)]
    ownf, msgf, cstf, fstat = tiles(far, [z], None, at_far)
    up[3], down[3], ownf, msg01 = hold((up[3], down[3], ownf, msg01))
    msgf = move(msgf, cell=1)
    own23, msg23, cst23 = tiles(([ordered], []), [pieces(2), pieces(3)], rstat, at_two, True)
    msg23 = move(msg23, cell=1)

    half = ownf.shape[0]
    (back,) = call(
        back_kernel, [((half, 256), jnp.int16)], [], 1 << 33, at_end, ownf, msgf, cstf, fstat
    )
    back = move(back, y=2)

    (result,) = call(
        functools.partial(final_kernel, ((0, 1), (2, 3))),
        [((half, 8, 128), jnp.float32)],
        [],
        1 << 24,
        at_end,
        *(rstat, back, own01, msg01, cst01, own23, msg23, cst23),
    )
    return result.reshape(half, 1, 1024)


def solution(mesh):
    fine = Mesh(mesh.devices.reshape(DIMS), AXES)
    return jax.shard_map(
        local,
        mesh=fine,
        in_specs=(P(AXES[:4], "cell"), P("cell"), P(), P(), P()),
        out_specs=P(("z", "y", "cell"), ("x", "core"), None),
        check_vma=False,
    )
```

```python
import functools
import math

import jax
import jax.numpy as jnp
import numpy as np
from jax import lax
from jax.experimental import pallas as pl
from jax.experimental.pallas import tpu as pltpu
from jax.sharding import Mesh
from jax.sharding import PartitionSpec as P

AXES = ("z", "y", "x", "core", "cell")
DIMS = (4, 4, 4, 2, 2)
NZ, NY, NX, NC, NH = DIMS
EPS = 1e-05
FULL = 32767.0
BOUND = 96.0
NT = (((1,), (1,)), ((), ()))


def move(value, **steps):
    step, pairs = [steps.get(axis, 0) for axis in AXES], []
    for i in range(math.prod(DIMS)):
        to = [(int(a) + s) % d for a, s, d in zip(np.unravel_index(i, DIMS), step, DIMS)]
        pairs.append((i, int(np.ravel_multi_index(to, DIMS))))
    return lax.ppermute(value, AXES, pairs)


def spread_x(copies):
    return lax.all_to_all(copies, "x", 0, 0, tiled=True)


def resid_kernel(limit, place, order, counts, size, mean, disp, out, copies, turned):
    genes = out.shape[0]
    block = order[place[0]]
    line = block * genes // 128
    start = pl.multiple_of(block * genes % 128, genes)
    both = [ref[pl.ds(line, 1), :] for ref in (mean, disp)]
    index = lax.broadcasted_iota(jnp.int32, (8, 128), 0)
    turned[...] = jnp.where(index == 0, both[0], both[1]).T
    mean_gene = turned[pl.ds(start, genes), 0:1]
    spare = 1.0 / turned[pl.ds(start, genes), 1:2]
    for i in range(0, out.shape[1], 512):
        span = slice(i, i + 512)
        expected = mean_gene * size[:, span]
        scale = lax.rsqrt(expected + expected * expected * spare)
        value = (counts[:, span].astype(jnp.float32) - expected) * scale
        value = jnp.clip(value, -limit, limit).astype(jnp.bfloat16)
        out[:, span] = value
        for j in range(NX):
            copies[genes * j : genes * j + genes, span] = value


def residuals(counts, size_factors, gene_means, dispersions, block_order):
    genes, cells = counts.shape
    place = lax.axis_index(AXES[:4]).astype(jnp.int32)
    smem, vmem = pl.BlockSpec(memory_space=pltpu.SMEM), pl.BlockSpec(memory_space=pltpu.VMEM)
    return pl.pallas_call(
        functools.partial(resid_kernel, math.sqrt(cells * NH)),
        in_specs=[smem, smem, vmem, vmem, vmem, vmem],
        out_specs=[vmem, vmem],
        out_shape=[
            jax.ShapeDtypeStruct((genes, cells), jnp.bfloat16),
            jax.ShapeDtypeStruct((NX * genes, cells), jnp.bfloat16),
        ],
        scratch_shapes=[pltpu.VMEM((128, 8), jnp.float32)],
        compiler_params=pltpu.CompilerParams(vmem_limit_bytes=VMEM_LIMIT),
    )(
        place[None],
        block_order,
        counts,
        size_factors[None, :],
        gene_means.reshape(-1, 128),
        dispersions.reshape(-1, 128),
    )


def encode(p):
    root = jnp.minimum(jnp.sqrt(jnp.abs(p)), 1.0) * FULL + 0.5
    return jnp.where(p < 0, -root, root).astype(jnp.int32).astype(jnp.int16)


def decode(q):
    f = q.astype(jnp.int32).astype(jnp.float32)
    return f * jnp.abs(f) * (1.0 / (FULL * FULL))


def split(v):
    t = v * (FULL / BOUND)
    high = jnp.round(t)
    return high, jnp.round((t - high) * (2 * FULL))


def unsplit(high, low):
    return (high + low * (0.5 / FULL)) * (BOUND / FULL)


def pack(rows):
    index = lax.broadcasted_iota(jnp.int32, (16, rows[0].shape[1]), 0)
    block = jnp.zeros(index.shape, jnp.float32)
    for i, row in enumerate(rows):
        block = jnp.where(index == i, row, block)
    return block.astype(jnp.int32).astype(jnp.int16)


def lane_sums(parts):
    ones = jnp.ones((8, 128), jnp.float32)
    return lax.dot_general(
        ones, parts, NT, precision=lax.Precision.HIGHEST, preferred_element_type=jnp.float32
    )[0:1, :]


def fold(values):
    tiles = [values[:, i : i + 128] for i in range(0, values.shape[1], 128)]
    while len(tiles) > 1:
        tiles = [a + b for a, b in zip(tiles[::2], tiles[1::2])]
    return tiles[0]


def deviation(square, mean):
    return jnp.sqrt(square - mean * mean + EPS)


def tile_kernel(cells, chunks, pieces, parts, first, export, at, *refs):
    refs = list(refs)
    blocks = [refs.pop(0) for _ in range(pieces)]
    rows = [refs.pop(0) for _ in range(1 + parts[-1][0] if parts else 1)]
    given = None if first else refs.pop(0)
    own, msg, cst = refs.pop(0), refs.pop(0), refs.pop(0)
    rst = refs.pop(0) if first else given
    ordered = refs.pop(0) if export else None
    rbuf = refs.pop(0) if parts else rows[0]
    cbuf, acc, sems = refs[:3]
    half = own.shape[0]
    width = cells // chunks
    block_at = [pl.ds(64 * i, 64) for i in range(pieces)]

    def copies(k):
        cells_k = pl.ds(width * k, width)
        pairs = [(p.at[:, cells_k], cbuf.at[span, cells_k]) for p, span in zip(blocks, block_at)]
        for i, (ref, start, size) in enumerate(parts):
            span = pl.ds(pl.multiple_of(at[1 + i] * 32, 32), size)
            pairs.append((rows[ref].at[pl.ds(start, size), cells_k], rbuf.at[span, cells_k]))
        made = [pltpu.make_async_copy(*pair, sems.at[k, i]) for i, pair in enumerate(pairs)]
        for copy in made:
            copy.start()
        return made

    flight = [copies(0), copies(1)] if parts else [[]] * chunks
    if not parts:
        for p, span in zip(blocks, block_at):
            cbuf[span, :] = p[...]
    used = 64 * pieces
    if used < cbuf.shape[0]:
        cbuf[used:, :] = jnp.zeros((cbuf.shape[0] - used, cells), cbuf.dtype)
    total = sums = squares = row_sums = row_squares = 0.0
    for k in range(chunks):
        for copy in flight[k]:
            copy.wait()
        if parts and k + 2 < chunks:
            flight.append(copies(k + 2))
        cells_k = slice(width * k, width * k + width)
        r, c = rbuf[:, cells_k], cbuf[:, cells_k]
        total += lax.dot_general(r, c, NT, preferred_element_type=jnp.float32)
        wide = c.astype(jnp.float32)
        sums += fold(wide)
        squares += fold(wide * wide)
        if first:
            wide = r.astype(jnp.float32)
            row_sums += fold(wide)
            row_squares += fold(wide * wide)
    if export:
        out = pltpu.make_async_copy(rbuf, ordered, sems.at[0, 0])
        out.start()
    acc[...] = total
    if first:
        refs[-2][...] = row_sums
        refs[-1][...] = row_squares

    scale = 1.0 / cells
    mine = pl.multiple_of(at[0] * half, half)
    other = pl.multiple_of((1 - at[0]) * half, half)
    extra = []
    if first:
        rs, rq = refs[-2:]
        mean = jnp.sum(rs[...], axis=1, keepdims=True) * scale
        dev = deviation(jnp.sum(rq[...], axis=1, keepdims=True) * scale, mean)
        lane = lax.broadcasted_iota(jnp.int32, rst.shape, 1)
        rst[...] = jnp.where(lane == 0, mean, dev)
        mean = lane_sums(rs[pl.ds(other, half), :]) * scale
        dev = deviation(lane_sums(rq[pl.ds(other, half), :]) * scale, mean)
        extra = [*split(mean), *split(dev)]
    mean = lane_sums(sums) * scale
    dev = deviation(lane_sums(squares) * scale, mean)
    row = lax.broadcasted_iota(jnp.int32, cst.shape, 0)
    cst[...] = jnp.where(row == 0, mean, dev)
    cov = acc[pl.ds(other, half), :] * scale - rst[pl.ds(other, half), 0:1] * mean
    msg[0:half, :] = encode(cov * ((1.0 / rst[pl.ds(other, half), 1:2]) * (1.0 / dev)))
    msg[half:, :] = pack([*split(mean), *split(dev), *extra])
    own[...] = acc[pl.ds(mine, half), :] * scale - rst[pl.ds(mine, half), 0:1] * mean
    if export:
        out.wait()


VMEM_LIMIT = 60 * 1024 * 1024
VMEM = pl.BlockSpec(memory_space=pltpu.VMEM)
SMEM = pl.BlockSpec(memory_space=pltpu.SMEM)
HBM = pl.BlockSpec(memory_space=pltpu.HBM)


class From:
    def __init__(self, table, first):
        self.table, self.first = table, first

    def __getitem__(self, i):
        return self.table[self.first + i]


def call(kernel, outs, scratch, flops, at, *args, places=None, out_places=None, limit=32 * 1024 * 1024):
    table, first = at
    return pl.pallas_call(
        lambda table, *refs: kernel(From(table, first), *refs),
        in_specs=[SMEM] + (places or [VMEM] * len(args)),
        out_specs=out_places or [VMEM] * len(outs),
        out_shape=[jax.ShapeDtypeStruct(*o) for o in outs],
        scratch_shapes=scratch,
        compiler_params=pltpu.CompilerParams(vmem_limit_bytes=limit or VMEM_LIMIT),
        cost_estimate=pl.CostEstimate(flops=flops, bytes_accessed=1 << 20, transcendentals=0),
    )(table, *args)


def tiles(rows, pieces, rstat, at, export=False, limit=None):
    rows, parts = rows
    n, cells = sum(part.shape[0] for part in rows), rows[0].shape[1]
    half, first, chunks = n // 2, rstat is None, 4
    wide = -(-len(pieces) // 2) * 128
    outs = [((half, wide), jnp.float32), ((half + 16, wide), jnp.int16), ((8, wide), jnp.float32)]
    out_places = [VMEM] * 3
    scratch = [pltpu.VMEM((n, cells), jnp.bfloat16)] if parts else []
    scratch += [
        pltpu.VMEM((wide, cells), jnp.bfloat16),
        pltpu.VMEM((n, wide), jnp.float32),
        pltpu.SemaphoreType.DMA((chunks, len(pieces) + len(parts))),
    ]
    if first:
        outs.append(((n, 128), jnp.float32))
        out_places.append(VMEM)
        scratch += [pltpu.VMEM((n, 128), jnp.float32)] * 2
    if export:
        outs.append(((n, cells), jnp.bfloat16))
        out_places.append(HBM)
    return call(
        functools.partial(tile_kernel, cells, chunks, len(pieces), parts, first, export),
        outs,
        scratch,
        int(1.15e9 * (2.5 + wide / 170 + (3.5 if parts else 0))),
        at,
        *pieces,
        *rows,
        *([] if first else [rstat]),
        places=[HBM if parts else VMEM] * (len(rows) + len(pieces)) + ([] if first else [VMEM]),
        out_places=out_places,
        limit=limit or (VMEM_LIMIT if parts else 32 * 1024 * 1024),
    )


def merged(mean, mean2, dev, dev2):
    gap = mean - mean2
    inv = lax.rsqrt(0.5 * (dev * dev + dev2 * dev2) + 0.25 * gap * gap)
    return inv, dev2 * inv, gap * inv


def received(block, i):
    f = block.astype(jnp.int32).astype(jnp.float32)
    return unsplit(f[i : i + 1, :], f[i + 1 : i + 2, :]), unsplit(f[i + 2 : i + 3, :], f[i + 3 : i + 4, :])


def row_factors(rst, block, half_id):
    mean2, dev2 = received(block, 4)
    index = lax.broadcasted_iota(jnp.int32, (8, mean2.shape[1]), 0)
    flip = jnp.where(index == 0, mean2, dev2).T
    half = flip.shape[0]
    mine = pl.multiple_of(half_id * half, half)
    own = rst[pl.ds(mine, half), :]
    return merged(own[:, 0:1], flip[:, 0:1], own[:, 1:2], flip[:, 1:2])


def joined(own, msg, cst, factors):
    half = own.shape[0]
    mean2, dev2 = received(msg[half : half + 16, :], 0)
    u, v, w = merged(cst[0:1, :], mean2, cst[1:2, :], dev2)
    ru, rv, rw = factors
    return (
        0.5 * own * (ru * u) + 0.5 * decode(msg[0:half, :]) * (rv * v) + 0.25 * (rw * w)
    )


def back_kernel(at, own, msg, cst, rst, out):
    half = own.shape[0]
    factors = row_factors(rst, msg[half : half + 16, :], at[0])
    out[...] = encode(joined(own[...], msg[...], cst[...], factors))


def final_kernel(groups, at, rst, back, *refs):
    out = refs[-1]
    half = back.shape[0]
    factors = row_factors(rst, refs[1][half:, :], at[0])
    far_all = decode(back[...])
    lane = lax.broadcasted_iota(jnp.int32, (1, 128), 1) // 64
    for g, ids in enumerate(groups):
        own, msg, cst = refs[3 * g : 3 * g + 3]
        values = joined(own[...], msg[...], cst[...], factors)
        for t, k in enumerate(ids):
            blocks = [values[:, 192 * t + 64 * i : 192 * t + 64 * i + 64] for i in range(3)]
            blocks.append(far_all[:, 64 * k : 64 * k + 64])
            twice = [jnp.concatenate([block, block], axis=1) for block in blocks]
            for i in range(2):
                which = (lane + (2 * i + 1 + NY - at[1])) % NY
                value = twice[3]
                for source in range(3):
                    value = jnp.where(which == source, twice[source], value)
                out[:, at[2 + k] * 2 + i, :] = value


def local(counts, size_factors, gene_means, dispersions, block_order):
    zl, y, x, c, h = [lax.axis_index(axis) for axis in AXES]
    hold = lax.optimization_barrier
    up, down = {}, {}
    place = lambda at, core: 2 * (NC * (at % NX) + core)
    lists = [
        [h] + [place(i, core) for core in (c, 1 - c) for i in range(NX)],
        [h] + [place(x + d, core) for core in (c, 1 - c) for d in (0, -1, 1, 2)],
        [h, y] + [(zl - k) % NZ for k in range(NZ)],
    ]
    table = jnp.stack([jnp.asarray(v, jnp.int32) for values in lists for v in values])
    starts = np.cumsum([0] + [len(values) for values in lists]).tolist()

    a, copies = residuals(counts, size_factors, gene_means, dispersions, block_order)

    far, z1 = move(a, y=2), move(a, z=1)
    rows = spread_x(copies)
    a, far, z1, table = hold((a, far, z1, table))
    at_near, at_far, at_end = [(table, start) for start in starts[:3]]

    up[0], down[0], z2 = move(a, y=1), move(a, y=-1), move(z1, z=1)
    right, left = move(far, x=1), move(far, x=-1)
    a, rows, z2, up[0], down[0], right, left = hold((a, rows, z2, up[0], down[0], right, left))

    pieces = lambda k: [up[k], z[k], down[k]]
    up[1], down[1], z3 = move(z1, y=1), move(z1, y=-1), move(a, z=3)
    z = [a, z1, z2, z3]
    across, rows_c = move(far, x=2), move(rows, core=1)
    rows = (rows, rows_c), [(i // NX, 64 * (i % NX), 64) for i in range(2 * NX)]
    own0, msg0, cst0, rstat, ordered = tiles(rows, pieces(0) + [a], None, at_near, True)
    z3, up[1], down[1], far, right, left, across, own0 = hold(
        (z3, up[1], down[1], far, right, left, across, own0)
    )

    z = [a, z1, z2, z3]
    up[2], down[2] = move(z2, y=1), move(z2, y=-1)
    far = jnp.concatenate([far, right, left, across], axis=0)
    far_c = move(far, core=1)
    msg0 = move(msg0, cell=1)
    own1, msg1, cst1 = tiles(rows, pieces(1), rstat, at_near)
    z3, up[2], down[2], msg0, own1, far, far_c = hold((z3, up[2], down[2], msg0, own1, far, far_c))

    z = [a, z1, z2, z3]
    up[3], down[3] = move(z3, y=1), move(z3, y=-1)
    msg1 = move(msg1, cell=1)
    ownf, msgf, cstf, fstat = tiles(((far, far_c), rows[1]), z, None, at_far, limit=48 * 1024 * 1024)
    up[3], down[3], ownf = hold((up[3], down[3], ownf))
    msgf = move(msgf, cell=1)
    own23, msg23, cst23 = tiles(([ordered], []), pieces(2) + pieces(3), rstat, at_near)
    msg23 = move(msg23, cell=1)

    half = ownf.shape[0]
    (back,) = call(
        back_kernel, [((half, 256), jnp.int16)], [], 1 << 33, at_end, ownf, msgf, cstf, fstat
    )
    back = move(back, y=2)

    (result,) = call(
        functools.partial(final_kernel, ((0,), (1,), (2, 3))),
        [((half, 8, 128), jnp.float32)],
        [],
        1 << 24,
        at_end,
        *(rstat, back, own0, msg0, cst0, own1, msg1, cst1, own23, msg23, cst23),
    )
    return result.reshape(half, 1, 1024)


def solution(mesh):
    fine = Mesh(mesh.devices.reshape(DIMS), AXES)
    return jax.shard_map(
        local,
        mesh=fine,
        in_specs=(P(AXES[:4], "cell"), P("cell"), P(), P(), P()),
        out_specs=P(("z", "y", "cell"), ("x", "core"), None),
        check_vma=False,
    )
```

```python
import functools
import math

import jax
import jax.numpy as jnp
import numpy as np
from jax import lax
from jax.experimental import pallas as pl
from jax.experimental.pallas import tpu as pltpu
from jax.sharding import Mesh
from jax.sharding import PartitionSpec as P

AXES = ("z", "y", "x", "core", "cell")
DIMS = (4, 4, 4, 2, 2)
NZ, NY, NX, NC, NH = DIMS
EPS = 1e-05
FULL = 32767.0
BOUND = 96.0
NT = (((1,), (1,)), ((), ()))


def move(value, **steps):
    step, pairs = [steps.get(axis, 0) for axis in AXES], []
    for i in range(math.prod(DIMS)):
        to = [(int(a) + s) % d for a, s, d in zip(np.unravel_index(i, DIMS), step, DIMS)]
        pairs.append((i, int(np.ravel_multi_index(to, DIMS))))
    return lax.ppermute(value, AXES, pairs)


def spread_x(copies):
    return lax.all_to_all(copies, "x", 0, 0, tiled=True)


def resid_kernel(limit, place, order, counts, size, mean, disp, out, copies, turned):
    genes = out.shape[0]
    block = order[place[0]]
    line = block * genes // 128
    start = pl.multiple_of(block * genes % 128, genes)
    both = [ref[pl.ds(line, 1), :] for ref in (mean, disp)]
    index = lax.broadcasted_iota(jnp.int32, (8, 128), 0)
    turned[...] = jnp.where(index == 0, both[0], both[1]).T
    mean_gene = turned[pl.ds(start, genes), 0:1]
    spare = 1.0 / turned[pl.ds(start, genes), 1:2]
    for i in range(0, out.shape[1], 512):
        span = slice(i, i + 512)
        expected = mean_gene * size[:, span]
        scale = lax.rsqrt(expected + expected * expected * spare)
        value = (counts[:, span].astype(jnp.float32) - expected) * scale
        value = jnp.clip(value, -limit, limit).astype(jnp.bfloat16)
        out[:, span] = value
        for j in range(NX):
            copies[genes * j : genes * j + genes, span] = value


def residuals(counts, size_factors, gene_means, dispersions, block_order):
    genes, cells = counts.shape
    place = lax.axis_index(AXES[:4]).astype(jnp.int32)
    smem, vmem = pl.BlockSpec(memory_space=pltpu.SMEM), pl.BlockSpec(memory_space=pltpu.VMEM)
    return pl.pallas_call(
        functools.partial(resid_kernel, math.sqrt(cells * NH)),
        in_specs=[smem, smem, vmem, vmem, vmem, vmem],
        out_specs=[vmem, vmem],
        out_shape=[
            jax.ShapeDtypeStruct((genes, cells), jnp.bfloat16),
            jax.ShapeDtypeStruct((NX * genes, cells), jnp.bfloat16),
        ],
        scratch_shapes=[pltpu.VMEM((128, 8), jnp.float32)],
        compiler_params=pltpu.CompilerParams(vmem_limit_bytes=VMEM_LIMIT),
    )(
        place[None],
        block_order,
        counts,
        size_factors[None, :],
        gene_means.reshape(-1, 128),
        dispersions.reshape(-1, 128),
    )


def encode(p):
    root = jnp.minimum(jnp.sqrt(jnp.abs(p)), 1.0) * FULL + 0.5
    return jnp.where(p < 0, -root, root).astype(jnp.int32).astype(jnp.int16)


def decode(q):
    f = q.astype(jnp.int32).astype(jnp.float32)
    return f * jnp.abs(f) * (1.0 / (FULL * FULL))


def split(v):
    t = v * (FULL / BOUND)
    high = jnp.round(t)
    return high, jnp.round((t - high) * (2 * FULL))


def unsplit(high, low):
    return (high + low * (0.5 / FULL)) * (BOUND / FULL)


def pack(rows):
    index = lax.broadcasted_iota(jnp.int32, (16, rows[0].shape[1]), 0)
    block = jnp.zeros(index.shape, jnp.float32)
    for i, row in enumerate(rows):
        block = jnp.where(index == i, row, block)
    return block.astype(jnp.int32).astype(jnp.int16)


def lane_sums(parts):
    ones = jnp.ones((8, 128), jnp.float32)
    return lax.dot_general(
        ones, parts, NT, precision=lax.Precision.HIGHEST, preferred_element_type=jnp.float32
    )[0:1, :]


def fold(values):
    tiles = [values[:, i : i + 128] for i in range(0, values.shape[1], 128)]
    while len(tiles) > 1:
        tiles = [a + b for a, b in zip(tiles[::2], tiles[1::2])]
    return tiles[0]


def deviation(square, mean):
    return jnp.sqrt(square - mean * mean + EPS)


def tile_kernel(cells, chunks, pieces, parts, first, export, at, *refs):
    refs = list(refs)
    blocks = [refs.pop(0) for _ in range(pieces)]
    rows = [refs.pop(0) for _ in range(1 + parts[-1][0] if parts else 1)]
    given = None if first else refs.pop(0)
    own, msg, cst = refs.pop(0), refs.pop(0), refs.pop(0)
    rst = refs.pop(0) if first else given
    ordered = refs.pop(0) if export else None
    rbuf = refs.pop(0) if parts else rows[0]
    cbuf, acc, sems = refs[:3]
    half = own.shape[0]
    width = cells // chunks
    block_at = [pl.ds(64 * i, 64) for i in range(pieces)]

    def copies(k):
        cells_k = pl.ds(width * k, width)
        pairs = [(p.at[:, cells_k], cbuf.at[span, cells_k]) for p, span in zip(blocks, block_at)]
        for i, (ref, start, size) in enumerate(parts):
            span = pl.ds(pl.multiple_of(at[1 + i] * 32, 32), size)
            pairs.append((rows[ref].at[pl.ds(start, size), cells_k], rbuf.at[span, cells_k]))
        made = [pltpu.make_async_copy(*pair, sems.at[k, i]) for i, pair in enumerate(pairs)]
        for copy in made:
            copy.start()
        return made

    flight = [copies(0), copies(1)] if parts else [[]] * chunks
    if not parts:
        for p, span in zip(blocks, block_at):
            cbuf[span, :] = p[...]
    used = 64 * pieces
    if used < cbuf.shape[0]:
        cbuf[used:, :] = jnp.zeros((cbuf.shape[0] - used, cells), cbuf.dtype)
    total = sums = squares = row_sums = row_squares = 0.0
    for k in range(chunks):
        for copy in flight[k]:
            copy.wait()
        if parts and k + 2 < chunks:
            flight.append(copies(k + 2))
        cells_k = slice(width * k, width * k + width)
        r, c = rbuf[:, cells_k], cbuf[:, cells_k]
        total += lax.dot_general(r, c, NT, preferred_element_type=jnp.float32)
        wide = c.astype(jnp.float32)
        sums += fold(wide)
        squares += fold(wide * wide)
        if first:
            wide = r.astype(jnp.float32)
            row_sums += fold(wide)
            row_squares += fold(wide * wide)
    if export:
        out = pltpu.make_async_copy(rbuf, ordered, sems.at[0, 0])
        out.start()
    acc[...] = total
    if first:
        refs[-2][...] = row_sums
        refs[-1][...] = row_squares

    scale = 1.0 / cells
    mine = pl.multiple_of(at[0] * half, half)
    other = pl.multiple_of((1 - at[0]) * half, half)
    extra = []
    if first:
        rs, rq = refs[-2:]
        mean = jnp.sum(rs[...], axis=1, keepdims=True) * scale
        dev = deviation(jnp.sum(rq[...], axis=1, keepdims=True) * scale, mean)
        lane = lax.broadcasted_iota(jnp.int32, rst.shape, 1)
        rst[...] = jnp.where(lane == 0, mean, dev)
        mean = lane_sums(rs[pl.ds(other, half), :]) * scale
        dev = deviation(lane_sums(rq[pl.ds(other, half), :]) * scale, mean)
        extra = [*split(mean), *split(dev)]
        spare = msg.shape[1] - half
        if spare:
            extra = [jnp.concatenate([e, jnp.zeros((1, spare), jnp.float32)], axis=1) for e in extra]
    mean = lane_sums(sums) * scale
    dev = deviation(lane_sums(squares) * scale, mean)
    row = lax.broadcasted_iota(jnp.int32, cst.shape, 0)
    cst[...] = jnp.where(row == 0, mean, dev)
    cov = acc[pl.ds(other, half), :] * scale - rst[pl.ds(other, half), 0:1] * mean
    msg[0:half, :] = encode(cov * ((1.0 / rst[pl.ds(other, half), 1:2]) * (1.0 / dev)))
    msg[half:, :] = pack([*split(mean), *split(dev), *extra])
    own[...] = acc[pl.ds(mine, half), :] * scale - rst[pl.ds(mine, half), 0:1] * mean
    if export:
        out.wait()


VMEM_LIMIT = 60 * 1024 * 1024
VMEM = pl.BlockSpec(memory_space=pltpu.VMEM)
SMEM = pl.BlockSpec(memory_space=pltpu.SMEM)
HBM = pl.BlockSpec(memory_space=pltpu.HBM)


class From:
    def __init__(self, table, first):
        self.table, self.first = table, first

    def __getitem__(self, i):
        return self.table[self.first + i]


def call(kernel, outs, scratch, flops, at, *args, places=None, out_places=None, limit=32 * 1024 * 1024):
    table, first = at
    return pl.pallas_call(
        lambda table, *refs: kernel(From(table, first), *refs),
        in_specs=[SMEM] + (places or [VMEM] * len(args)),
        out_specs=out_places or [VMEM] * len(outs),
        out_shape=[jax.ShapeDtypeStruct(*o) for o in outs],
        scratch_shapes=scratch,
        compiler_params=pltpu.CompilerParams(vmem_limit_bytes=limit or VMEM_LIMIT),
        cost_estimate=pl.CostEstimate(flops=flops, bytes_accessed=1 << 20, transcendentals=0),
    )(table, *args)


def tiles(rows, pieces, rstat, at, export=False, limit=None):
    rows, parts = rows
    n, cells = sum(part.shape[0] for part in rows), rows[0].shape[1]
    half, first, chunks = n // 2, rstat is None, 4
    wide = -(-len(pieces) // 2) * 128
    outs = [((half, wide), jnp.float32), ((half + 16, wide), jnp.int16), ((8, wide), jnp.float32)]
    out_places = [VMEM] * 3
    scratch = [pltpu.VMEM((n, cells), jnp.bfloat16)] if parts else []
    scratch += [
        pltpu.VMEM((wide, cells), jnp.bfloat16),
        pltpu.VMEM((n, wide), jnp.float32),
        pltpu.SemaphoreType.DMA((chunks, len(pieces) + len(parts))),
    ]
    if first:
        outs.append(((n, 128), jnp.float32))
        out_places.append(VMEM)
        scratch += [pltpu.VMEM((n, 128), jnp.float32)] * 2
    if export:
        outs.append(((n, cells), jnp.bfloat16))
        out_places.append(HBM)
    return call(
        functools.partial(tile_kernel, cells, chunks, len(pieces), parts, first, export),
        outs,
        scratch,
        int(1.15e9 * (2.5 + wide / 170 + (3.5 if parts else 0))),
        at,
        *pieces,
        *rows,
        *([] if first else [rstat]),
        places=[HBM if parts else VMEM] * (len(rows) + len(pieces)) + ([] if first else [VMEM]),
        out_places=out_places,
        limit=limit or (VMEM_LIMIT if parts else 32 * 1024 * 1024),
    )


def merged(mean, mean2, dev, dev2):
    gap = mean - mean2
    inv = lax.rsqrt(0.5 * (dev * dev + dev2 * dev2) + 0.25 * gap * gap)
    return inv, dev2 * inv, gap * inv


def received(block, i):
    f = block.astype(jnp.int32).astype(jnp.float32)
    return unsplit(f[i : i + 1, :], f[i + 1 : i + 2, :]), unsplit(f[i + 2 : i + 3, :], f[i + 3 : i + 4, :])


def row_factors(rst, block, half_id):
    mean2, dev2 = received(block, 4)
    mean2, dev2 = mean2[:, : rst.shape[0] // 2], dev2[:, : rst.shape[0] // 2]
    index = lax.broadcasted_iota(jnp.int32, (8, mean2.shape[1]), 0)
    flip = jnp.where(index == 0, mean2, dev2).T
    half = flip.shape[0]
    mine = pl.multiple_of(half_id * half, half)
    own = rst[pl.ds(mine, half), :]
    return merged(own[:, 0:1], flip[:, 0:1], own[:, 1:2], flip[:, 1:2])


def joined(own, msg, cst, factors):
    half = own.shape[0]
    mean2, dev2 = received(msg[half : half + 16, :], 0)
    u, v, w = merged(cst[0:1, :], mean2, cst[1:2, :], dev2)
    ru, rv, rw = factors
    return (
        0.5 * own * (ru * u) + 0.5 * decode(msg[0:half, :]) * (rv * v) + 0.25 * (rw * w)
    )


def back_kernel(at, own, msg, cst, rst, out):
    half = own.shape[0]
    factors = row_factors(rst, msg[half : half + 16, :], at[0])
    out[...] = encode(joined(own[...], msg[...], cst[...], factors))


def final_kernel(groups, at, rst, back, *refs):
    out = refs[-1]
    half = back.shape[0]
    factors = row_factors(rst, refs[1][half:, :], at[0])
    far_all = decode(back[...])
    lane = lax.broadcasted_iota(jnp.int32, (1, 128), 1) // 64
    for g, ids in enumerate(groups):
        own, msg, cst = refs[3 * g : 3 * g + 3]
        values = joined(own[...], msg[...], cst[...], factors)
        for t, k in enumerate(ids):
            blocks = [values[:, 192 * t + 64 * i : 192 * t + 64 * i + 64] for i in range(3)]
            blocks.append(far_all[:, 64 * k : 64 * k + 64])
            twice = [jnp.concatenate([block, block], axis=1) for block in blocks]
            for i in range(2):
                which = (lane + (2 * i + 1 + NY - at[1])) % NY
                value = twice[3]
                for source in range(3):
                    value = jnp.where(which == source, twice[source], value)
                out[:, at[2 + k] * 2 + i, :] = value


def local(counts, size_factors, gene_means, dispersions, block_order):
    zl, y, x, c, h = [lax.axis_index(axis) for axis in AXES]
    hold = lax.optimization_barrier
    up, down = {}, {}
    place = lambda at, core: 2 * (NC * (at % NX) + core)
    lists = [
        [h] + [place(i, core) for core in (c, 1 - c) for i in range(NX)],
        [h] + [place(x + d, core) for core in (c, 1 - c) for d in (0, -1, 1, 2)],
        [h, y] + [(zl - k) % NZ for k in range(NZ)],
    ]
    table = jnp.stack([jnp.asarray(v, jnp.int32) for values in lists for v in values])
    starts = np.cumsum([0] + [len(values) for values in lists]).tolist()

    a, copies = residuals(counts, size_factors, gene_means, dispersions, block_order)

    up[0], down[0], z1, far = move(a, y=1), move(a, y=-1), move(a, z=1), move(a, y=2)
    z3 = move(a, z=3)
    rows = spread_x(copies)
    up[0], down[0], z1, z3, far, table = hold((up[0], down[0], z1, z3, far, table))
    at_near, at_far, at_end = [(table, start) for start in starts[:3]]

    up[1], down[1], z2 = move(z1, y=1), move(z1, y=-1), move(z1, z=1)
    far, far_c = hold((far, move(far, core=1)))
    right, left = move(far, x=1), move(far, x=-1)
    rows, z2, up[1], down[1], right, left = hold((rows, z2, up[1], down[1], right, left))

    pieces = lambda k: [up[k], z[k], down[k]]
    z = [a, z1, z2, z3]
    up[2], down[2] = move(z2, y=1), move(z2, y=-1)
    rows_c, across = move(rows, core=1), move(far, x=2)
    rows = (rows, rows_c), [(i // NX, 64 * (i % NX), 64) for i in range(2 * NX)]
    own01, msg01, cst01, rstat, ordered = tiles(
        rows, pieces(0) + pieces(1), None, at_near, True
    )
    z3, up[2], down[2], own01, across = hold((z3, up[2], down[2], own01, across))

    z = [a, z1, z2, z3]
    up[3], down[3] = move(z3, y=1), move(z3, y=-1)
    across_c, right_c, left_c = move(across, core=1), move(right, core=1), move(left, core=1)
    msg01 = move(msg01, cell=1)
    far = [far, right, left, across, far_c, right_c, left_c, across_c]
    far = far, [(i, 0, 64) for i in range(len(far))]
    ownf, msgf, cstf, fstat = tiles(far, z, None, at_far, limit=48 * 1024 * 1024)
    up[3], down[3], ownf = hold((up[3], down[3], ownf))
    msgf = move(msgf, cell=1)
    own23, msg23, cst23 = tiles(([ordered], []), pieces(2) + pieces(3), rstat, at_near)
    msg23 = move(msg23, cell=1)

    half = ownf.shape[0]
    (back,) = call(
        back_kernel, [((half, 256), jnp.int16)], [], 1 << 33, at_end, ownf, msgf, cstf, fstat
    )
    back = move(back, y=2)

    (result,) = call(
        functools.partial(final_kernel, ((0, 1), (2, 3))),
        [((half, 8, 128), jnp.float32)],
        [],
        1 << 24,
        at_end,
        *(rstat, back, own01, msg01, cst01, own23, msg23, cst23),
    )
    return result.reshape(half, 1, 1024)


def solution(mesh):
    fine = Mesh(mesh.devices.reshape(DIMS), AXES)
    return jax.shard_map(
        local,
        mesh=fine,
        in_specs=(P(AXES[:4], "cell"), P("cell"), P(), P(), P()),
        out_specs=P(("z", "y", "cell"), ("x", "core"), None),
        check_vma=False,
    )
```

```python
import functools
import math

import jax
import jax.numpy as jnp
import numpy as np
from jax import lax
from jax.experimental import pallas as pl
from jax.experimental.pallas import tpu as pltpu
from jax.sharding import Mesh
from jax.sharding import PartitionSpec as P

AXES = ("z", "y", "x", "core", "cell")
DIMS = (4, 4, 4, 2, 2)
NZ, NY, NX, NC, NH = DIMS
EPS = 1e-05
FULL = 32767.0
BOUND = 96.0
NT = (((1,), (1,)), ((), ()))


def move(value, **steps):
    step, pairs = [steps.get(axis, 0) for axis in AXES], []
    for i in range(math.prod(DIMS)):
        to = [(int(a) + s) % d for a, s, d in zip(np.unravel_index(i, DIMS), step, DIMS)]
        pairs.append((i, int(np.ravel_multi_index(to, DIMS))))
    return lax.ppermute(value, AXES, pairs)


def spread_x(copies):
    return lax.all_to_all(copies, "x", 0, 0, tiled=True)


def resid_kernel(limit, place, order, counts, size, mean, disp, out, copies, turned):
    genes = out.shape[0]
    block = order[place[0]]
    line = block * genes // 128
    start = pl.multiple_of(block * genes % 128, genes)
    both = [ref[pl.ds(line, 1), :] for ref in (mean, disp)]
    index = lax.broadcasted_iota(jnp.int32, (8, 128), 0)
    turned[...] = jnp.where(index == 0, both[0], both[1]).T
    mean_gene = turned[pl.ds(start, genes), 0:1]
    spare = 1.0 / turned[pl.ds(start, genes), 1:2]
    for i in range(0, out.shape[1], 512):
        span = slice(i, i + 512)
        expected = mean_gene * size[:, span]
        scale = lax.rsqrt(expected + expected * expected * spare)
        value = (counts[:, span].astype(jnp.float32) - expected) * scale
        value = jnp.clip(value, -limit, limit).astype(jnp.bfloat16)
        out[:, span] = value
        for j in range(NX):
            copies[genes * j : genes * j + genes, span] = value


def residuals(counts, size_factors, gene_means, dispersions, block_order):
    genes, cells = counts.shape
    place = lax.axis_index(AXES[:4]).astype(jnp.int32)
    smem, vmem = pl.BlockSpec(memory_space=pltpu.SMEM), pl.BlockSpec(memory_space=pltpu.VMEM)
    return pl.pallas_call(
        functools.partial(resid_kernel, math.sqrt(cells * NH)),
        in_specs=[smem, smem, vmem, vmem, vmem, vmem],
        out_specs=[vmem, vmem],
        out_shape=[
            jax.ShapeDtypeStruct((genes, cells), jnp.bfloat16),
            jax.ShapeDtypeStruct((NX * genes, cells), jnp.bfloat16),
        ],
        scratch_shapes=[pltpu.VMEM((128, 8), jnp.float32)],
        compiler_params=pltpu.CompilerParams(vmem_limit_bytes=VMEM_LIMIT),
    )(
        place[None],
        block_order,
        counts,
        size_factors[None, :],
        gene_means.reshape(-1, 128),
        dispersions.reshape(-1, 128),
    )


def encode(p):
    root = jnp.minimum(jnp.sqrt(jnp.abs(p)), 1.0) * FULL + 0.5
    return jnp.where(p < 0, -root, root).astype(jnp.int32).astype(jnp.int16)


def decode(q):
    f = q.astype(jnp.int32).astype(jnp.float32)
    return f * jnp.abs(f) * (1.0 / (FULL * FULL))


def split(v):
    t = v * (FULL / BOUND)
    high = jnp.round(t)
    return high, jnp.round((t - high) * (2 * FULL))


def unsplit(high, low):
    return (high + low * (0.5 / FULL)) * (BOUND / FULL)


def pack(rows):
    index = lax.broadcasted_iota(jnp.int32, (16, rows[0].shape[1]), 0)
    block = jnp.zeros(index.shape, jnp.float32)
    for i, row in enumerate(rows):
        block = jnp.where(index == i, row, block)
    return block.astype(jnp.int32).astype(jnp.int16)


def lane_sums(parts):
    ones = jnp.ones((8, 128), jnp.float32)
    return lax.dot_general(
        ones, parts, NT, precision=lax.Precision.HIGHEST, preferred_element_type=jnp.float32
    )[0:1, :]


def fold(values):
    tiles = [values[:, i : i + 128] for i in range(0, values.shape[1], 128)]
    while len(tiles) > 1:
        tiles = [a + b for a, b in zip(tiles[::2], tiles[1::2])]
    return tiles[0]


def deviation(square, mean):
    return jnp.sqrt(square - mean * mean + EPS)


def tile_kernel(cells, chunks, pieces, parts, first, export, at, *refs):
    refs = list(refs)
    blocks = [refs.pop(0) for _ in range(pieces)]
    rows = [refs.pop(0) for _ in range(1 + parts[-1][0] if parts else 1)]
    given = None if first else refs.pop(0)
    own, msg, cst = refs.pop(0), refs.pop(0), refs.pop(0)
    rst = refs.pop(0) if first else given
    ordered = refs.pop(0) if export else None
    rbuf = refs.pop(0) if parts else rows[0]
    cbuf, acc, sems = refs[:3]
    half = own.shape[0]
    width = cells // chunks
    block_at = [pl.ds(64 * i, 64) for i in range(pieces)]

    def copies(k):
        cells_k = pl.ds(width * k, width)
        pairs = [(p.at[:, cells_k], cbuf.at[span, cells_k]) for p, span in zip(blocks, block_at)]
        for i, (ref, start, size) in enumerate(parts):
            span = pl.ds(pl.multiple_of(at[1 + i] * 32, 32), size)
            pairs.append((rows[ref].at[pl.ds(start, size), cells_k], rbuf.at[span, cells_k]))
        made = [pltpu.make_async_copy(*pair, sems.at[k, i]) for i, pair in enumerate(pairs)]
        for copy in made:
            copy.start()
        return made

    flight = [copies(0), copies(1)] if parts else [[]] * chunks
    if not parts:
        for p, span in zip(blocks, block_at):
            cbuf[span, :] = p[...]
    used = 64 * pieces
    if used < cbuf.shape[0]:
        cbuf[used:, :] = jnp.zeros((cbuf.shape[0] - used, cells), cbuf.dtype)
    total = sums = squares = row_sums = row_squares = 0.0
    for k in range(chunks):
        for copy in flight[k]:
            copy.wait()
        if parts and k + 2 < chunks:
            flight.append(copies(k + 2))
        cells_k = slice(width * k, width * k + width)
        r, c = rbuf[:, cells_k], cbuf[:, cells_k]
        total += lax.dot_general(r, c, NT, preferred_element_type=jnp.float32)
        wide = c.astype(jnp.float32)
        sums += fold(wide)
        squares += fold(wide * wide)
        if first:
            wide = r.astype(jnp.float32)
            row_sums += fold(wide)
            row_squares += fold(wide * wide)
    if export:
        out = pltpu.make_async_copy(rbuf, ordered, sems.at[0, 0])
        out.start()
    acc[...] = total
    if first:
        refs[-2][...] = row_sums
        refs[-1][...] = row_squares

    scale = 1.0 / cells
    mine = pl.multiple_of(at[0] * half, half)
    other = pl.multiple_of((1 - at[0]) * half, half)
    extra = []
    if first:
        rs, rq = refs[-2:]
        mean = jnp.sum(rs[...], axis=1, keepdims=True) * scale
        dev = deviation(jnp.sum(rq[...], axis=1, keepdims=True) * scale, mean)
        lane = lax.broadcasted_iota(jnp.int32, rst.shape, 1)
        rst[...] = jnp.where(lane == 0, mean, dev)
        mean = lane_sums(rs[pl.ds(other, half), :]) * scale
        dev = deviation(lane_sums(rq[pl.ds(other, half), :]) * scale, mean)
        extra = [*split(mean), *split(dev)]
        spare = msg.shape[1] - half
        if spare:
            extra = [jnp.concatenate([e, jnp.zeros((1, spare), jnp.float32)], axis=1) for e in extra]
    mean = lane_sums(sums) * scale
    dev = deviation(lane_sums(squares) * scale, mean)
    row = lax.broadcasted_iota(jnp.int32, cst.shape, 0)
    cst[...] = jnp.where(row == 0, mean, dev)
    cov = acc[pl.ds(other, half), :] * scale - rst[pl.ds(other, half), 0:1] * mean
    msg[0:half, :] = encode(cov * ((1.0 / rst[pl.ds(other, half), 1:2]) * (1.0 / dev)))
    msg[half:, :] = pack([*split(mean), *split(dev), *extra])
    own[...] = acc[pl.ds(mine, half), :] * scale - rst[pl.ds(mine, half), 0:1] * mean
    if export:
        out.wait()


VMEM_LIMIT = 60 * 1024 * 1024
VMEM = pl.BlockSpec(memory_space=pltpu.VMEM)
SMEM = pl.BlockSpec(memory_space=pltpu.SMEM)
HBM = pl.BlockSpec(memory_space=pltpu.HBM)


class From:
    def __init__(self, table, first):
        self.table, self.first = table, first

    def __getitem__(self, i):
        return self.table[self.first + i]


def call(kernel, outs, scratch, flops, at, *args, places=None, out_places=None, limit=32 * 1024 * 1024):
    table, first = at
    return pl.pallas_call(
        lambda table, *refs: kernel(From(table, first), *refs),
        in_specs=[SMEM] + (places or [VMEM] * len(args)),
        out_specs=out_places or [VMEM] * len(outs),
        out_shape=[jax.ShapeDtypeStruct(*o) for o in outs],
        scratch_shapes=scratch,
        compiler_params=pltpu.CompilerParams(vmem_limit_bytes=limit or VMEM_LIMIT),
        cost_estimate=pl.CostEstimate(flops=flops, bytes_accessed=1 << 20, transcendentals=0),
    )(table, *args)


def tiles(rows, pieces, rstat, at, export=False, limit=None):
    rows, parts = rows
    n, cells = sum(part.shape[0] for part in rows), rows[0].shape[1]
    half, first, chunks = n // 2, rstat is None, 4
    wide = -(-len(pieces) // 2) * 128
    outs = [((half, wide), jnp.float32), ((half + 16, wide), jnp.int16), ((8, wide), jnp.float32)]
    out_places = [VMEM] * 3
    scratch = [pltpu.VMEM((n, cells), jnp.bfloat16)] if parts else []
    scratch += [
        pltpu.VMEM((wide, cells), jnp.bfloat16),
        pltpu.VMEM((n, wide), jnp.float32),
        pltpu.SemaphoreType.DMA((chunks, len(pieces) + len(parts))),
    ]
    if first:
        outs.append(((n, 128), jnp.float32))
        out_places.append(VMEM)
        scratch += [pltpu.VMEM((n, 128), jnp.float32)] * 2
    if export:
        outs.append(((n, cells), jnp.bfloat16))
        out_places.append(HBM)
    return call(
        functools.partial(tile_kernel, cells, chunks, len(pieces), parts, first, export),
        outs,
        scratch,
        int(1.15e9 * (2.5 + wide / 170 + (3.5 if parts else 0))),
        at,
        *pieces,
        *rows,
        *([] if first else [rstat]),
        places=[HBM if parts else VMEM] * (len(rows) + len(pieces)) + ([] if first else [VMEM]),
        out_places=out_places,
        limit=limit or (VMEM_LIMIT if parts else 32 * 1024 * 1024),
    )


def merged(mean, mean2, dev, dev2):
    gap = mean - mean2
    inv = lax.rsqrt(0.5 * (dev * dev + dev2 * dev2) + 0.25 * gap * gap)
    return inv, dev2 * inv, gap * inv


def received(block, i):
    f = block.astype(jnp.int32).astype(jnp.float32)
    return unsplit(f[i : i + 1, :], f[i + 1 : i + 2, :]), unsplit(f[i + 2 : i + 3, :], f[i + 3 : i + 4, :])


def row_factors(rst, block, half_id):
    mean2, dev2 = received(block, 4)
    mean2, dev2 = mean2[:, : rst.shape[0] // 2], dev2[:, : rst.shape[0] // 2]
    index = lax.broadcasted_iota(jnp.int32, (8, mean2.shape[1]), 0)
    flip = jnp.where(index == 0, mean2, dev2).T
    half = flip.shape[0]
    mine = pl.multiple_of(half_id * half, half)
    own = rst[pl.ds(mine, half), :]
    return merged(own[:, 0:1], flip[:, 0:1], own[:, 1:2], flip[:, 1:2])


def joined(own, msg, cst, factors):
    half = own.shape[0]
    mean2, dev2 = received(msg[half : half + 16, :], 0)
    u, v, w = merged(cst[0:1, :], mean2, cst[1:2, :], dev2)
    ru, rv, rw = factors
    return (
        0.5 * own * (ru * u) + 0.5 * decode(msg[0:half, :]) * (rv * v) + 0.25 * (rw * w)
    )


def back_kernel(at, own, msg, cst, rst, out):
    half = own.shape[0]
    factors = row_factors(rst, msg[half : half + 16, :], at[0])
    out[...] = encode(joined(own[...], msg[...], cst[...], factors))


def final_kernel(groups, at, rst, back, *refs):
    out = refs[-1]
    half = back.shape[0]
    factors = row_factors(rst, refs[1][half:, :], at[0])
    far_all = decode(back[...])
    lane = lax.broadcasted_iota(jnp.int32, (1, 128), 1) // 64
    for g, ids in enumerate(groups):
        own, msg, cst = refs[3 * g : 3 * g + 3]
        values = joined(own[...], msg[...], cst[...], factors)
        for t, k in enumerate(ids):
            blocks = [values[:, 192 * t + 64 * i : 192 * t + 64 * i + 64] for i in range(3)]
            blocks.append(far_all[:, 64 * k : 64 * k + 64])
            twice = [jnp.concatenate([block, block], axis=1) for block in blocks]
            for i in range(2):
                which = (lane + (2 * i + 1 + NY - at[1])) % NY
                value = twice[3]
                for source in range(3):
                    value = jnp.where(which == source, twice[source], value)
                out[:, at[2 + k] * 2 + i, :] = value


def local(counts, size_factors, gene_means, dispersions, block_order):
    zl, y, x, c, h = [lax.axis_index(axis) for axis in AXES]
    hold = lax.optimization_barrier
    up, down = {}, {}
    place = lambda at, core: 2 * (NC * (at % NX) + core)
    lists = [
        [h] + [place(i, core) for core in (c, 1 - c) for i in range(NX)],
        [h] + [place(x + d, core) for core in (c, 1 - c) for d in (0, -1, 1, 2)],
        [h, y] + [(zl - k) % NZ for k in range(NZ)],
    ]
    table = jnp.stack([jnp.asarray(v, jnp.int32) for values in lists for v in values])
    starts = np.cumsum([0] + [len(values) for values in lists]).tolist()

    a, copies = residuals(counts, size_factors, gene_means, dispersions, block_order)

    up[0], down[0], z1, far = move(a, y=1), move(a, y=-1), move(a, z=1), move(a, y=2)
    rows = spread_x(copies)
    a, up[0], down[0], z1, far, table = hold((a, up[0], down[0], z1, far, table))
    at_near, at_far, at_end = [(table, start) for start in starts[:3]]

    up[1], down[1], z2 = move(z1, y=1), move(z1, y=-1), move(z1, z=1)
    far, far_c = hold((far, move(far, core=1)))
    right, left = move(far, x=1), move(far, x=-1)
    a, rows, z2, up[1], down[1], right, left = hold((a, rows, z2, up[1], down[1], right, left))
    z3 = move(a, z=3)

    pieces = lambda k: [up[k], z[k], down[k]]
    z = [a, z1, z2, z3]
    up[2], down[2] = move(z2, y=1), move(z2, y=-1)
    rows_c, across = move(rows, core=1), move(far, x=2)
    rows = (rows, rows_c), [(i // NX, 64 * (i % NX), 64) for i in range(2 * NX)]
    own01, msg01, cst01, rstat, ordered = tiles(
        rows, pieces(0) + pieces(1), None, at_near, True
    )
    z3, up[2], down[2], own01, across = hold((z3, up[2], down[2], own01, across))

    z = [a, z1, z2, z3]
    up[3], down[3] = move(z3, y=1), move(z3, y=-1)
    across_c, right_c, left_c = move(across, core=1), move(right, core=1), move(left, core=1)
    msg01 = move(msg01, cell=1)
    far = [far, right, left, across, far_c, right_c, left_c, across_c]
    far = far, [(i, 0, 64) for i in range(len(far))]
    ownf, msgf, cstf, fstat = tiles(far, z, None, at_far, limit=48 * 1024 * 1024)
    up[3], down[3], ownf = hold((up[3], down[3], ownf))
    msgf = move(msgf, cell=1)
    own23, msg23, cst23 = tiles(([ordered], []), pieces(2) + pieces(3), rstat, at_near)
    msg23 = move(msg23, cell=1)

    half = ownf.shape[0]
    (back,) = call(
        back_kernel, [((half, 256), jnp.int16)], [], 1 << 33, at_end, ownf, msgf, cstf, fstat
    )
    back = move(back, y=2)

    (result,) = call(
        functools.partial(final_kernel, ((0, 1), (2, 3))),
        [((half, 8, 128), jnp.float32)],
        [],
        1 << 24,
        at_end,
        *(rstat, back, own01, msg01, cst01, own23, msg23, cst23),
    )
    return result.reshape(half, 1, 1024)


def solution(mesh):
    fine = Mesh(mesh.devices.reshape(DIMS), AXES)
    return jax.shard_map(
        local,
        mesh=fine,
        in_specs=(P(AXES[:4], "cell"), P("cell"), P(), P(), P()),
        out_specs=P(("z", "y", "cell"), ("x", "core"), None),
        check_vma=False,
    )
```

```python
import functools
import math

import jax
import jax.numpy as jnp
import numpy as np
from jax import lax
from jax.experimental import pallas as pl
from jax.experimental.pallas import tpu as pltpu
from jax.sharding import Mesh
from jax.sharding import PartitionSpec as P

AXES = ("z", "y", "x", "core", "cell")
DIMS = (4, 4, 4, 2, 2)
NZ, NY, NX, NC, NH = DIMS
EPS = 1e-05
FULL = 32767.0
BOUND = 96.0
NT = (((1,), (1,)), ((), ()))


def move(value, **steps):
    step, pairs = [steps.get(axis, 0) for axis in AXES], []
    for i in range(math.prod(DIMS)):
        to = [(int(a) + s) % d for a, s, d in zip(np.unravel_index(i, DIMS), step, DIMS)]
        pairs.append((i, int(np.ravel_multi_index(to, DIMS))))
    return lax.ppermute(value, AXES, pairs)


def spread_x(copies):
    return lax.all_to_all(copies, "x", 0, 0, tiled=True)


def resid_kernel(limit, place, order, counts, size, mean, disp, out, copies, turned):
    genes = out.shape[0]
    block = order[place[0]]
    line = block * genes // 128
    start = pl.multiple_of(block * genes % 128, genes)
    both = [ref[pl.ds(line, 1), :] for ref in (mean, disp)]
    index = lax.broadcasted_iota(jnp.int32, (8, 128), 0)
    turned[...] = jnp.where(index == 0, both[0], both[1]).T
    mean_gene = turned[pl.ds(start, genes), 0:1]
    spare = 1.0 / turned[pl.ds(start, genes), 1:2]
    for i in range(0, out.shape[1], 512):
        span = slice(i, i + 512)
        expected = mean_gene * size[:, span]
        scale = lax.rsqrt(expected + expected * expected * spare)
        value = (counts[:, span].astype(jnp.float32) - expected) * scale
        value = jnp.clip(value, -limit, limit).astype(jnp.bfloat16)
        out[:, span] = value
        for j in range(NX):
            copies[genes * j : genes * j + genes, span] = value


def residuals(counts, size_factors, gene_means, dispersions, block_order):
    genes, cells = counts.shape
    place = lax.axis_index(AXES[:4]).astype(jnp.int32)
    smem, vmem = pl.BlockSpec(memory_space=pltpu.SMEM), pl.BlockSpec(memory_space=pltpu.VMEM)
    return pl.pallas_call(
        functools.partial(resid_kernel, math.sqrt(cells * NH)),
        in_specs=[smem, smem, vmem, vmem, vmem, vmem],
        out_specs=[vmem, vmem],
        out_shape=[
            jax.ShapeDtypeStruct((genes, cells), jnp.bfloat16),
            jax.ShapeDtypeStruct((NX * genes, cells), jnp.bfloat16),
        ],
        scratch_shapes=[pltpu.VMEM((128, 8), jnp.float32)],
        compiler_params=pltpu.CompilerParams(vmem_limit_bytes=VMEM_LIMIT),
    )(
        place[None],
        block_order,
        counts,
        size_factors[None, :],
        gene_means.reshape(-1, 128),
        dispersions.reshape(-1, 128),
    )


def encode(p):
    root = jnp.minimum(jnp.sqrt(jnp.abs(p)), 1.0) * FULL + 0.5
    return jnp.where(p < 0, -root, root).astype(jnp.int32).astype(jnp.int16)


def decode(q):
    f = q.astype(jnp.int32).astype(jnp.float32)
    return f * jnp.abs(f) * (1.0 / (FULL * FULL))


def split(v):
    t = v * (FULL / BOUND)
    high = jnp.round(t)
    return high, jnp.round((t - high) * (2 * FULL))


def unsplit(high, low):
    return (high + low * (0.5 / FULL)) * (BOUND / FULL)


def pack(rows):
    index = lax.broadcasted_iota(jnp.int32, (16, rows[0].shape[1]), 0)
    block = jnp.zeros(index.shape, jnp.float32)
    for i, row in enumerate(rows):
        block = jnp.where(index == i, row, block)
    return block.astype(jnp.int32).astype(jnp.int16)


def lane_sums(parts):
    ones = jnp.ones((8, 128), jnp.float32)
    return lax.dot_general(
        ones, parts, NT, precision=lax.Precision.HIGHEST, preferred_element_type=jnp.float32
    )[0:1, :]


def fold(values):
    tiles = [values[:, i : i + 128] for i in range(0, values.shape[1], 128)]
    while len(tiles) > 1:
        tiles = [a + b for a, b in zip(tiles[::2], tiles[1::2])]
    return tiles[0]


def deviation(square, mean):
    return jnp.sqrt(square - mean * mean + EPS)


def tile_kernel(cells, chunks, pieces, parts, first, export, at, *refs):
    refs = list(refs)
    blocks = [refs.pop(0) for _ in range(pieces)]
    rows = [refs.pop(0) for _ in range(1 + parts[-1][0] if parts else 1)]
    given = None if first else refs.pop(0)
    own, msg, cst = refs.pop(0), refs.pop(0), refs.pop(0)
    rst = refs.pop(0) if first else given
    ordered = refs.pop(0) if export else None
    rbuf = refs.pop(0) if parts else rows[0]
    cbuf, acc, sems = refs[:3]
    half = own.shape[0]
    width = cells // chunks
    block_at = [pl.ds(64 * i, 64) for i in range(pieces)]

    def copies(k):
        cells_k = pl.ds(width * k, width)
        pairs = [(p.at[:, cells_k], cbuf.at[span, cells_k]) for p, span in zip(blocks, block_at)]
        for i, (ref, start, size) in enumerate(parts):
            span = pl.ds(pl.multiple_of(at[1 + i] * 32, 32), size)
            pairs.append((rows[ref].at[pl.ds(start, size), cells_k], rbuf.at[span, cells_k]))
        made = [pltpu.make_async_copy(*pair, sems.at[k, i]) for i, pair in enumerate(pairs)]
        for copy in made:
            copy.start()
        return made

    flight = [copies(0), copies(1)] if parts else [[]] * chunks
    if not parts:
        for p, span in zip(blocks, block_at):
            cbuf[span, :] = p[...]
    used = 64 * pieces
    if used < cbuf.shape[0]:
        cbuf[used:, :] = jnp.zeros((cbuf.shape[0] - used, cells), cbuf.dtype)
    total = sums = squares = row_sums = row_squares = 0.0
    for k in range(chunks):
        for copy in flight[k]:
            copy.wait()
        if parts and k + 2 < chunks:
            flight.append(copies(k + 2))
        cells_k = slice(width * k, width * k + width)
        r, c = rbuf[:, cells_k], cbuf[:, cells_k]
        total += lax.dot_general(r, c, NT, preferred_element_type=jnp.float32)
        wide = c.astype(jnp.float32)
        sums += fold(wide)
        squares += fold(wide * wide)
        if first:
            wide = r.astype(jnp.float32)
            row_sums += fold(wide)
            row_squares += fold(wide * wide)
    if export:
        out = pltpu.make_async_copy(rbuf, ordered, sems.at[0, 0])
        out.start()
    acc[...] = total
    if first:
        refs[-2][...] = row_sums
        refs[-1][...] = row_squares

    scale = 1.0 / cells
    mine = pl.multiple_of(at[0] * half, half)
    other = pl.multiple_of((1 - at[0]) * half, half)
    extra = []
    if first:
        rs, rq = refs[-2:]
        mean = jnp.sum(rs[...], axis=1, keepdims=True) * scale
        dev = deviation(jnp.sum(rq[...], axis=1, keepdims=True) * scale, mean)
        lane = lax.broadcasted_iota(jnp.int32, rst.shape, 1)
        rst[...] = jnp.where(lane == 0, mean, dev)
        mean = lane_sums(rs[pl.ds(other, half), :]) * scale
        dev = deviation(lane_sums(rq[pl.ds(other, half), :]) * scale, mean)
        extra = [*split(mean), *split(dev)]
        spare = msg.shape[1] - half
        if spare:
            extra = [jnp.concatenate([e, jnp.zeros((1, spare), jnp.float32)], axis=1) for e in extra]
    mean = lane_sums(sums) * scale
    dev = deviation(lane_sums(squares) * scale, mean)
    row = lax.broadcasted_iota(jnp.int32, cst.shape, 0)
    cst[...] = jnp.where(row == 0, mean, dev)
    cov = acc[pl.ds(other, half), :] * scale - rst[pl.ds(other, half), 0:1] * mean
    msg[0:half, :] = encode(cov * ((1.0 / rst[pl.ds(other, half), 1:2]) * (1.0 / dev)))
    msg[half:, :] = pack([*split(mean), *split(dev), *extra])
    own[...] = acc[pl.ds(mine, half), :] * scale - rst[pl.ds(mine, half), 0:1] * mean
    if export:
        out.wait()


VMEM_LIMIT = 60 * 1024 * 1024
VMEM = pl.BlockSpec(memory_space=pltpu.VMEM)
SMEM = pl.BlockSpec(memory_space=pltpu.SMEM)
HBM = pl.BlockSpec(memory_space=pltpu.HBM)


class From:
    def __init__(self, table, first):
        self.table, self.first = table, first

    def __getitem__(self, i):
        return self.table[self.first + i]


def call(kernel, outs, scratch, flops, at, *args, places=None, out_places=None, limit=32 * 1024 * 1024):
    table, first = at
    return pl.pallas_call(
        lambda table, *refs: kernel(From(table, first), *refs),
        in_specs=[SMEM] + (places or [VMEM] * len(args)),
        out_specs=out_places or [VMEM] * len(outs),
        out_shape=[jax.ShapeDtypeStruct(*o) for o in outs],
        scratch_shapes=scratch,
        compiler_params=pltpu.CompilerParams(vmem_limit_bytes=limit or VMEM_LIMIT),
        cost_estimate=pl.CostEstimate(flops=flops, bytes_accessed=1 << 20, transcendentals=0),
    )(table, *args)


def tiles(rows, pieces, rstat, at, export=False, limit=None):
    rows, parts = rows
    n, cells = sum(part.shape[0] for part in rows), rows[0].shape[1]
    half, first, chunks = n // 2, rstat is None, 4
    wide = -(-len(pieces) // 2) * 128
    outs = [((half, wide), jnp.float32), ((half + 16, wide), jnp.int16), ((8, wide), jnp.float32)]
    out_places = [VMEM] * 3
    scratch = [pltpu.VMEM((n, cells), jnp.bfloat16)] if parts else []
    scratch += [
        pltpu.VMEM((wide, cells), jnp.bfloat16),
        pltpu.VMEM((n, wide), jnp.float32),
        pltpu.SemaphoreType.DMA((chunks, len(pieces) + len(parts))),
    ]
    if first:
        outs.append(((n, 128), jnp.float32))
        out_places.append(VMEM)
        scratch += [pltpu.VMEM((n, 128), jnp.float32)] * 2
    if export:
        outs.append(((n, cells), jnp.bfloat16))
        out_places.append(HBM)
    return call(
        functools.partial(tile_kernel, cells, chunks, len(pieces), parts, first, export),
        outs,
        scratch,
        int(1.15e9 * (2.5 + wide / 170 + (3.5 if parts else 0))),
        at,
        *pieces,
        *rows,
        *([] if first else [rstat]),
        places=[HBM if parts else VMEM] * (len(rows) + len(pieces)) + ([] if first else [VMEM]),
        out_places=out_places,
        limit=limit or (VMEM_LIMIT if parts else 32 * 1024 * 1024),
    )


def merged(mean, mean2, dev, dev2):
    gap = mean - mean2
    inv = lax.rsqrt(0.5 * (dev * dev + dev2 * dev2) + 0.25 * gap * gap)
    return inv, dev2 * inv, gap * inv


def received(block, i):
    f = block.astype(jnp.int32).astype(jnp.float32)
    return unsplit(f[i : i + 1, :], f[i + 1 : i + 2, :]), unsplit(f[i + 2 : i + 3, :], f[i + 3 : i + 4, :])


def row_factors(rst, block, half_id):
    mean2, dev2 = received(block, 4)
    mean2, dev2 = mean2[:, : rst.shape[0] // 2], dev2[:, : rst.shape[0] // 2]
    index = lax.broadcasted_iota(jnp.int32, (8, mean2.shape[1]), 0)
    flip = jnp.where(index == 0, mean2, dev2).T
    half = flip.shape[0]
    mine = pl.multiple_of(half_id * half, half)
    own = rst[pl.ds(mine, half), :]
    return merged(own[:, 0:1], flip[:, 0:1], own[:, 1:2], flip[:, 1:2])


def joined(own, msg, cst, factors):
    half = own.shape[0]
    mean2, dev2 = received(msg[half : half + 16, :], 0)
    u, v, w = merged(cst[0:1, :], mean2, cst[1:2, :], dev2)
    ru, rv, rw = factors
    return (
        0.5 * own * (ru * u) + 0.5 * decode(msg[0:half, :]) * (rv * v) + 0.25 * (rw * w)
    )


def back_kernel(at, own, msg, cst, rst, out):
    half = own.shape[0]
    factors = row_factors(rst, msg[half : half + 16, :], at[0])
    out[...] = encode(joined(own[...], msg[...], cst[...], factors))


def final_kernel(groups, at, rst, back, *refs):
    out = refs[-1]
    half = back.shape[0]
    factors = row_factors(rst, refs[1][half:, :], at[0])
    far_all = decode(back[...])
    lane = lax.broadcasted_iota(jnp.int32, (1, 128), 1) // 64
    for g, ids in enumerate(groups):
        own, msg, cst = refs[3 * g : 3 * g + 3]
        values = joined(own[...], msg[...], cst[...], factors)
        for t, k in enumerate(ids):
            blocks = [values[:, 192 * t + 64 * i : 192 * t + 64 * i + 64] for i in range(3)]
            blocks.append(far_all[:, 64 * k : 64 * k + 64])
            twice = [jnp.concatenate([block, block], axis=1) for block in blocks]
            for i in range(2):
                which = (lane + (2 * i + 1 + NY - at[1])) % NY
                value = twice[3]
                for source in range(3):
                    value = jnp.where(which == source, twice[source], value)
                out[:, at[2 + k] * 2 + i, :] = value


def local(counts, size_factors, gene_means, dispersions, block_order):
    zl, y, x, c, h = [lax.axis_index(axis) for axis in AXES]
    hold = lax.optimization_barrier
    up, down = {}, {}
    place = lambda at, core: 2 * (NC * (at % NX) + core)
    lists = [
        [h] + [place(i, core) for core in (c, 1 - c) for i in range(NX)],
        [h] + [place(x + d, core) for core in (c, 1 - c) for d in (0, -1, 1, 2)],
        [h, y] + [(zl - k) % NZ for k in range(NZ)],
    ]
    table = jnp.stack([jnp.asarray(v, jnp.int32) for values in lists for v in values])
    starts = np.cumsum([0] + [len(values) for values in lists]).tolist()

    a, copies = residuals(counts, size_factors, gene_means, dispersions, block_order)

    up[0], down[0], z1, far = move(a, y=1), move(a, y=-1), move(a, z=1), move(a, y=2)
    rows = spread_x(copies)
    a, up[0], down[0], z1, far, table = hold((a, up[0], down[0], z1, far, table))
    at_near, at_far, at_end = [(table, start) for start in starts[:3]]

    up[1], down[1], z2 = move(z1, y=1), move(z1, y=-1), move(z1, z=1)
    far, far_c = hold((far, move(far, core=1)))
    right, left = move(far, x=1), move(far, x=-1)
    a, rows, z2, up[1], down[1], right, left = hold((a, rows, z2, up[1], down[1], right, left))
    z3 = move(a, z=3)

    pieces = lambda k: [up[k], z[k], down[k]]
    z = [a, z1, z2, z3]
    up[2], down[2] = move(z2, y=1), move(z2, y=-1)
    rows_c, across = move(rows, core=1), move(far, x=2)
    rows = (rows, rows_c), [(i // NX, 64 * (i % NX), 64) for i in range(2 * NX)]
    own01, msg01, cst01, rstat, ordered = tiles(
        rows, pieces(0) + pieces(1), None, at_near, True
    )
    z3, up[2], down[2], own01, right, left, across = hold(
        (z3, up[2], down[2], own01, right, left, across)
    )

    z = [a, z1, z2, z3]
    up[3], down[3] = move(z3, y=1), move(z3, y=-1)
    across_c, right_c, left_c = move(across, core=1), move(right, core=1), move(left, core=1)
    msg01 = move(msg01, cell=1)
    far = [far, right, left, across, far_c, right_c, left_c, across_c]
    far = far, [(i, 0, 64) for i in range(len(far))]
    ownf, msgf, cstf, fstat = tiles(far, z, None, at_far, limit=48 * 1024 * 1024)
    up[3], down[3], ownf = hold((up[3], down[3], ownf))
    msgf = move(msgf, cell=1)
    own23, msg23, cst23 = tiles(([ordered], []), pieces(2) + pieces(3), rstat, at_near)
    msg23 = move(msg23, cell=1)

    half = ownf.shape[0]
    (back,) = call(
        back_kernel, [((half, 256), jnp.int16)], [], 1 << 33, at_end, ownf, msgf, cstf, fstat
    )
    back = move(back, y=2)

    (result,) = call(
        functools.partial(final_kernel, ((0, 1), (2, 3))),
        [((half, 8, 128), jnp.float32)],
        [],
        1 << 24,
        at_end,
        *(rstat, back, own01, msg01, cst01, own23, msg23, cst23),
    )
    return result.reshape(half, 1, 1024)


def solution(mesh):
    fine = Mesh(mesh.devices.reshape(DIMS), AXES)
    return jax.shard_map(
        local,
        mesh=fine,
        in_specs=(P(AXES[:4], "cell"), P("cell"), P(), P(), P()),
        out_specs=P(("z", "y", "cell"), ("x", "core"), None),
        check_vma=False,
    )
```
